256 devices in a mesh: wide: 64 (over y, z, core), orb: 4 (over x).
Axes of the slice: x: 4, y: 4, z: 8, core: 2. Of those that a mesh axis runs over, the one named last changes fastest.
Arguments:
- green_packed: bfloat16 [2, 64, 16, 256, 256], P(None, 'wide', 'orb'), may hold values from -6 to 6
- bubble_weight: float32 [16, 16], replicated, may hold values from -1.5 to 1.5
- tile_owner: int32 [64], replicated, may hold values from 0 to 63, as said below
- pairing: int32 [64], replicated, may hold values from 0 to 63, as said below
Outputs:
- response: bfloat16 [2, 64, 16, 256, 256], P(None, 'wide', 'orb')
The draws below stay inside these ranges and needn't reach their ends.
Inputs may be any that keep to these rules, and one draw needn't show every extreme that they name: `tile_owner`: A permutation of the 64 time tiles; slot s lies on index s // (8 * 8 / 64) of wide. The tiles in slots s and s + 32 are mirror images (tiles i * 8 + j and j * 8 + i) or both diagonal tiles. pairing[s] is the slot whose tile is the mirror image of tile_owner[s]: s itself for a diagonal tile, else the slot 32 away.
All inputs are finite; a program needn't handle non-finite values.
Results may differ from the reference program's by a relative error of at most 0.018.
Values may be sent and summed in bfloat16 or wider, within the bound.
A program may use at most 128 MiB of HBM per device.

```python
import jax
import jax.numpy as jnp
import numpy as np
from jax import lax

NORB = 4
NP = 16
K = 64
NT = 256
NTILE = 8
TS = 32


def mirror_units():
    leading = []
    trailing = []
    for upper_row in range(NTILE):
        for lower_row in range(upper_row + 1, NTILE):
            leading.append(upper_row * NTILE + lower_row)
            trailing.append(lower_row * NTILE + upper_row)
    for middle in range(NTILE // 2):
        leading.append(2 * middle * (NTILE + 1))
        trailing.append((2 * middle + 1) * (NTILE + 1))
    return (np.array(leading, np.int32), np.array(trailing, np.int32))


def slot_tables(key):
    leading, trailing = mirror_units()
    half_count = NTILE * NTILE // 2
    shuffled = jax.random.permutation(jax.random.fold_in(key, 71), half_count)
    flipped = jax.random.randint(jax.random.fold_in(key, 72), (half_count,), 0, 2)
    lead_tiles = jnp.asarray(leading)[shuffled]
    trail_tiles = jnp.asarray(trailing)[shuffled]
    upper_half = jnp.where(flipped == 1, trail_tiles, lead_tiles)
    lower_half = jnp.where(flipped == 1, lead_tiles, trail_tiles)
    owners = jnp.concatenate([upper_half, lower_half]).astype(jnp.int32)
    slot_ids = jnp.arange(2 * half_count, dtype=jnp.int32)
    diagonal = owners // NTILE == owners % NTILE
    partner = jnp.where(diagonal, slot_ids, (slot_ids + half_count) % (2 * half_count))
    return (owners, partner.astype(jnp.int32))


def draw_tile_owner(key, part):
    return slot_tables(key)[0]


def draw_pairing(key, part):
    return slot_tables(key)[1]


def levels(key, shape, split, low, high):
    gain, own = 1.0, jax.random.fold_in(key, 6)
    for dim, blocks in split:
        heights = jnp.exp(jax.random.uniform(jax.random.fold_in(own, dim), (blocks,), jnp.float32, low / len(split), high / len(split)))
        gain = gain * jnp.repeat(heights, shape[dim] // blocks).reshape([-1 if axis == dim else 1 for axis in range(len(shape))])
    return gain


def gaussian(stream_key, dims, scale, reach, split=(), held_as=jnp.bfloat16):
    values = scale * jax.random.normal(stream_key, dims, jnp.float32)
    if split:
        values = values * levels(stream_key, dims, split, -0.22, 0.18)
    return jnp.clip(values, -reach, reach).astype(held_as)


def setup_inputs(seed: int = 0) -> dict:
    key_of = jax.random.split(jax.random.key(seed), 5)
    return {
        "green_packed": gaussian(key_of[0], (2, K, NP, NT, NT), 1.0, 6.0, ((1, 64), (2, 4))),
        "bubble_weight": gaussian(key_of[1], (NP, NP), NP ** -0.5, 1.5, (), jnp.float32),
        "tile_owner": draw_tile_owner(jax.random.fold_in(key_of[4], 71), 0),
        "pairing": draw_pairing(jax.random.fold_in(key_of[4], 71), 0),
    }


precise = lax.Precision.HIGHEST


def complex_mix(former, latter):
    def single(first_op, second_op):
        return jnp.einsum("acts,cbsu->abtu", first_op, second_op, precision=precise)
    real_part = single(former[0], latter[0]) - single(former[1], latter[1])
    imag_part = single(former[0], latter[1]) + single(former[1], latter[0])
    return jnp.stack([real_part, imag_part], axis=0)


def reference(green_packed, bubble_weight, tile_owner, pairing):
    tile_area = TS * TS
    blocks = green_packed.reshape(2, K, NP, NTILE, TS, NTILE, TS).transpose(3, 5, 0, 1, 2, 4, 6)
    blocks = blocks.reshape(NTILE * NTILE, 2, K, NP, tile_area)
    group_weight = bubble_weight.astype(jnp.float32).reshape(NP, NORB, NORB)

    def to_real(tile_data):
        values = tile_data.astype(jnp.float32)
        spread = jnp.fft.ifft(lax.complex(values[0], values[1]), axis=0, norm="ortho")
        return jnp.stack([jnp.real(spread), jnp.imag(spread)], axis=0).astype(jnp.bfloat16)

    def slot_self(slot):
        own_tile = lax.dynamic_index_in_dim(blocks, tile_owner[slot].astype(jnp.int32), 0, keepdims=False)
        other_slot = pairing[slot].astype(jnp.int32)
        other_tile = lax.dynamic_index_in_dim(blocks, tile_owner[other_slot].astype(jnp.int32), 0, keepdims=False)
        real_green = to_real(own_tile)
        facing = to_real(other_tile)
        extent = facing.shape
        facing = jnp.swapaxes(facing.reshape(extent[:-1] + (TS, TS)), -1, -2).reshape(extent)
        mirror = jnp.roll(jnp.flip(facing, axis=1), 1, axis=1)
        own32 = real_green.astype(jnp.float32)
        mirror32 = mirror.astype(jnp.float32)
        product = jnp.stack([own32[0] * mirror32[0] - own32[1] * mirror32[1],
                             own32[0] * mirror32[1] + own32[1] * mirror32[0]], axis=0)
        grouped = product.reshape(2, K, NORB, NORB, tile_area)
        partial_value = jnp.einsum("qab,ckabx->ackqx", group_weight, grouped, precision=precise)
        partial_value = lax.optimization_barrier(partial_value.astype(jnp.bfloat16)).astype(jnp.float32)
        bubble = jnp.sum(partial_value, axis=0)
        self_re = own32[0] * bubble[0] - own32[1] * bubble[1]
        self_im = own32[0] * bubble[1] + own32[1] * bubble[0]
        back = jnp.fft.fft(lax.complex(self_re, self_im), axis=0, norm="ortho")
        return jnp.stack([jnp.real(back), jnp.imag(back)], axis=0).astype(jnp.bfloat16)

    self_slots = lax.map(slot_self, jnp.arange(NTILE * NTILE, dtype=jnp.int32))
    placed = jnp.zeros_like(self_slots).at[tile_owner].set(self_slots)
    self_energy = placed.reshape(NTILE, NTILE, 2, K, NP, TS, TS).transpose(2, 3, 4, 0, 5, 1, 6)
    self_energy = self_energy.reshape(2, K, NP, NT, NT)

    positions = jnp.arange(NT, dtype=jnp.int32)
    lower_mask = positions[:, None] >= positions[None, :]
    strict_lower = positions[:, None] > positions[None, :]
    conj_sign = jnp.array([1.0, -1.0], jnp.float32).reshape(2, 1, 1, 1, 1)

    def per_momentum(pieces):
        green_k, self_k = pieces
        green32 = green_k.astype(jnp.float32).reshape(2, NORB, NORB, NT, NT)
        self32 = self_k.astype(jnp.float32).reshape(2, NORB, NORB, NT, NT)
        swapped = green32.transpose(0, 2, 1, 4, 3)
        retarded_g = jnp.where(lower_mask, green32, 0.0)
        lesser_g = jnp.where(lower_mask, jnp.where(strict_lower, -conj_sign * swapped, 0.0), green32)
        advanced_g = jnp.where(strict_lower, 0.0, conj_sign * swapped)
        retarded_s = jnp.where(lower_mask, self32, 0.0)
        upper_s = jnp.where(lower_mask, 0.0, self32)
        retarded = complex_mix(retarded_s, retarded_g)
        lesser = complex_mix(retarded_s, lesser_g) + complex_mix(upper_s, advanced_g)
        combined = jnp.where(lower_mask, retarded, lesser) * (NT ** -0.5)
        return combined.reshape(2, NP, NT, NT).astype(jnp.bfloat16)

    response = lax.map(per_momentum, (jnp.moveaxis(green_packed, 1, 0), jnp.moveaxis(self_energy, 1, 0)))
    return jnp.moveaxis(response, 0, 1)
```

```python
import math

import jax
import jax.numpy as jnp
from jax import lax
from jax.experimental import pallas as pl
from jax.experimental.pallas import tpu as pltpu
from jax.sharding import PartitionSpec as P

NORB = 4
NT = 256
K = 64
HALF = 128
NDEV = 256

f32 = jnp.float32
bf16 = jnp.bfloat16


def shear(x, h):
    lane = lax.broadcasted_iota(jnp.int32, (NT, HALF), 1)
    if h:
        x = jnp.concatenate([x[HALF:], x[:HALF]], axis=0)
    for bit in (6, 5, 4, 3):
        m = 1 << bit
        y = x.reshape(NT // (2 * m), 2, m, HALF)
        swapped = jnp.concatenate([y[:, 1:2], y[:, 0:1]], axis=1).reshape(NT, HALF)
        x = jnp.where((lane & m) != 0, swapped, x)
    lane = lax.broadcasted_iota(jnp.int32, (NT // 8, 8, HALF), 2)
    row = lax.broadcasted_iota(jnp.int32, (NT // 8, 8, HALF), 1)
    x = x.reshape(NT // 8, 8, HALF)
    for bit in (2, 1, 0):
        m = 1 << bit
        swapped = pltpu.roll(x, m, 1)
        if bit < 2:
            swapped = jnp.where((row & m) != 0, swapped, pltpu.roll(x, 8 - m, 1))
        x = jnp.where((lane & m) != 0, swapped, x)
    return x.reshape(NT, HALF)


def add(u, v):
    return (u[0] + v[0], u[1] + v[1])


def sub(u, v):
    return (u[0] - v[0], u[1] - v[1])


def times(u, cr, ci):
    return (u[0] * cr - u[1] * ci, u[0] * ci + u[1] * cr)


def turn(u, sign):
    return (-u[1], u[0]) if sign > 0 else (u[1], -u[0])


def fft4(a, b, c, d, sign):
    t0, t1, t2, t3 = add(a, c), sub(a, c), add(b, d), turn(sub(b, d), sign)
    return [add(t0, t2), add(t1, t3), sub(t0, t2), sub(t1, t3)]


def fft8(x, sign):
    even = fft4(x[0], x[2], x[4], x[6], sign)
    odd = fft4(x[1], x[3], x[5], x[7], sign)
    c = math.sqrt(0.5)
    odd = [
        odd[0],
        ((odd[1][0] - sign * odd[1][1]) * c, (sign * odd[1][0] + odd[1][1]) * c),
        turn(odd[2], sign),
        ((-odd[3][0] - sign * odd[3][1]) * c, (sign * odd[3][0] - odd[3][1]) * c),
    ]
    return [add(e, o) for e, o in zip(even, odd)] + [sub(e, o) for e, o in zip(even, odd)]


def fft64(load, store, mid, sign):
    for k2 in range(8):
        y = fft8([load(8 * k1 + k2) for k1 in range(8)], sign)
        for r1 in range(8):
            v = y[r1]
            angle = 2.0 * math.pi * k2 * r1 / 64
            cr, ci = 0.125 * math.cos(angle), sign * 0.125 * math.sin(angle)
            v = times(v, cr, ci) if k2 * r1 else (v[0] * 0.125, v[1] * 0.125)
            mid[0, r1 * 8 + k2] = v[0]
            mid[1, r1 * 8 + k2] = v[1]
    for r1 in range(8):
        y = fft8([(mid[0, r1 * 8 + k2], mid[1, r1 * 8 + k2]) for k2 in range(8)], sign)
        for r2 in range(8):
            store(r1 + 8 * r2, y[r2])


def both_parts(tile):
    x = tile.astype(f32)
    return (x[:8], x[8:])


def tile_of(v):
    return jnp.concatenate([v[0], v[1]], axis=0).astype(bf16)


def kernel(
    x_ref, w_ref, o_ref, rows, snd, rcv, mid, rg, mir, self_real, wv, snd2, rcv2, g, rhs_r, rhs_la, lhs, s1, r1, s2, r2, s3, r3, s4
):
    orb = lax.axis_index("orb")
    wide = lax.axis_index("wide")
    me = wide * NORB + orb

    def place(d):
        return (d // NORB, d % NORB)

    def shear_plane(p, carry):
        c, b = p // 4, p % 4
        for h in range(2):
            x = x_ref[p, :, h * HALF : (h + 1) * HALF].astype(f32)
            rows[pl.ds(pl.multiple_of((c * 8 + h * 4 + b) * NT, NT), NT), :] = shear(x, h)
        return carry

    lax.fori_loop(0, 8, shear_plane, 0)

    def make_tile(e):
        snd[e] = tile_of((rows[pl.ds(e, 8, stride=NT), :], rows[pl.ds(8 * NT + e, 8, stride=NT), :]))

    def send(i, carry):
        d = (me + i) % NDEV
        make_tile(d)
        pltpu.make_async_remote_copy(snd.at[d], rcv.at[me], s1, r1, device_id=place(d)).start()
        return carry

    lax.fori_loop(1, NDEV, send, 0)
    make_tile(me)
    rcv[me] = snd[me]

    for i in range(1, NORB):
        pltpu.make_async_remote_copy(x_ref, g.at[orb], s2, r2, device_id=(wide, (orb + i) % NORB)).start()
    own = pltpu.make_async_copy(x_ref, g.at[orb], s4)
    own.start()

    sub8 = lax.broadcasted_iota(jnp.int32, (8, HALF), 0) % 4
    for a2 in range(4):
        for a in range(4):
            for j in range(4):
                v = jnp.full((8, HALF), w_ref[a2 * 4, a * 4 + j], f32)
                for b2 in range(1, 4):
                    v = jnp.where(sub8 == b2, w_ref[a2 * 4 + b2, a * 4 + (b2 + j) % 4], v)
                wv[(a2 * 4 + a) * 4 + j] = v

    arrived = pltpu.make_async_remote_copy(snd.at[pl.ds(0, NDEV - 1)], rcv.at[pl.ds(0, NDEV - 1)], s1, r1, device_id=(wide, orb))
    arrived.wait_recv()

    def to_sites(a, carry):
        def store(r, v):
            rg[r * NORB + a] = tile_of(v)

        fft64(lambda k: both_parts(rcv[k * NORB + a]), store, mid, 1)
        return carry

    lax.fori_loop(0, NORB, to_sites, 0)

    low = me % HALF
    i0 = lax.broadcasted_iota(jnp.int32, (HALF, HALF), 0)
    i1 = lax.broadcasted_iota(jnp.int32, (HALF, HALF), 1)
    perm = jnp.where(i0 == (i1 ^ low), 1.0, 0.0).astype(bf16)

    def mirror_rows(i, carry):
        block = rg[pl.ds(i * 32, 32)].reshape(512, HALF)
        out = jnp.dot(block, perm, preferred_element_type=f32)
        mir[pl.ds(i * 32, 32)] = out.astype(bf16).reshape(32, 16, HALF)
        return carry

    lax.fori_loop(0, 8, mirror_rows, 0)

    swap = (lax.broadcasted_iota(jnp.int32, (8, HALF), 0) * 0 + me // HALF) == 1

    def site(r, carry):
        back = (K - r) % K
        own_v, shifted = [], []
        for a in range(4):
            u = both_parts(rg[r * NORB + a])
            v = both_parts(mir[back * NORB + a])
            v = tuple(jnp.where(swap, pltpu.roll(z, 4, 0), z) for z in v)
            own_v.append(u)
            prod = (u[0] * v[0] - u[1] * v[1], u[0] * v[1] + u[1] * v[0])
            turned = [prod]
            for j in (1, 2, 3):
                turned.append(tuple(jnp.where(sub8 < 4 - j, pltpu.roll(z, 8 - j, 0), pltpu.roll(z, 4 - j, 0)) for z in prod))
            shifted.append(turned)
        for a2 in range(4):
            re = im = None
            for a in range(4):
                for j in range(4):
                    w = wv[(a2 * 4 + a) * 4 + j]
                    tr, ti = w * shifted[a][j][0], w * shifted[a][j][1]
                    re = tr if re is None else re + tr
                    im = ti if im is None else im + ti
            u = own_v[a2]
            self_real[0, r * NORB + a2] = u[0] * re - u[1] * im
            self_real[1, r * NORB + a2] = u[0] * im + u[1] * re
        return carry

    lax.fori_loop(0, K, site, 0)

    def to_momenta(i, carry):
        a = (orb + i) % NORB

        def store(k, v):
            snd2[k * NORB + a] = tile_of(v)

        fft64(lambda r: (self_real[0, r * NORB + a], self_real[1, r * NORB + a]), store, mid, -1)

        def send_back(n, carry):
            k = (wide + n) % K
            d = k * NORB + a

            @pl.when(d != me)
            def _():
                pltpu.make_async_remote_copy(snd2.at[d], rcv2.at[me], s3, r3, device_id=(k, a)).start()

            return carry

        lax.fori_loop(0, K, send_back, 0)
        return carry

    lax.fori_loop(0, NORB, to_momenta, 0)
    rcv2[me] = snd2[me]

    own.wait()
    gathered = pltpu.make_async_remote_copy(g.at[pl.ds(0, 3)], g.at[pl.ds(0, 3)], s2, r2, device_id=(wide, orb))
    gathered.wait_recv()
    ti = lax.broadcasted_iota(jnp.int32, (NT, NT), 0)
    ui = lax.broadcasted_iota(jnp.int32, (NT, NT), 1)

    def operands(i, carry):
        c, b = i // 4, i % 4
        for part in range(2):
            own_g = g[c, part * 4 + b].astype(f32)
            adjoint = g[b, part * 4 + c].astype(f32).T
            if part:
                adjoint = -adjoint
            n = c * 2 + part
            rhs_r[b, n] = jnp.where(ti >= ui, own_g, 0.0).astype(bf16)
            rhs_la[b, n] = jnp.where(ti < ui, own_g, jnp.where(ti > ui, -adjoint, 0.0)).astype(bf16)
            rhs_la[b, 8 + n] = jnp.where(ti <= ui, adjoint, 0.0).astype(bf16)
        return carry

    lax.fori_loop(0, 16, operands, 0)

    returned = pltpu.make_async_remote_copy(snd2.at[pl.ds(0, NDEV - 1)], rcv2.at[pl.ds(0, NDEV - 1)], s3, r3, device_id=(wide, orb))
    returned.wait_recv()

    def spread(e, carry):
        re, im = both_parts(rcv2[e])
        rows[pl.ds(e, 8, stride=NT), :] = re
        rows[pl.ds(8 * NT + e, 8, stride=NT), :] = im
        return carry

    lax.fori_loop(0, NDEV, spread, 0)

    def left(c, carry):
        for h in range(2):
            t_pos = lax.broadcasted_iota(jnp.int32, (NT, HALF), 0)
            s_pos = lax.broadcasted_iota(jnp.int32, (NT, HALF), 1) + h * HALF
            lower = t_pos >= s_pos
            for part in range(2):
                x = shear(rows[pl.ds(pl.multiple_of((part * 8 + h * 4 + c) * NT, NT), NT), :], h)
                ret = jnp.where(lower, x, 0.0)
                les = jnp.where(lower, 0.0, x)
                for off, z in ((0, ret), (8, les)):
                    same = pl.multiple_of((off + c * 2 + part) * NT, NT) + h * HALF
                    other = pl.multiple_of((off + c * 2 + 1 - part) * NT, NT) + h * HALF
                    if part == 0:
                        lhs[:NT, pl.ds(same, HALF)] = z.astype(bf16)
                        lhs[NT:, pl.ds(other, HALF)] = z.astype(bf16)
                    else:
                        lhs[:NT, pl.ds(same, HALF)] = (-z).astype(bf16)
                        lhs[NT:, pl.ds(other, HALF)] = z.astype(bf16)
        return carry

    lax.fori_loop(0, NORB, left, 0)

    def products(b, carry):
        ret = jnp.dot(lhs[:, : 8 * NT], rhs_r[b].reshape(8 * NT, NT), preferred_element_type=f32)
        les = jnp.dot(lhs[...], rhs_la[b].reshape(16 * NT, NT), preferred_element_type=f32)
        for part in range(2):
            sl = slice(part * NT, (part + 1) * NT)
            o_ref[part * 4 + b] = (jnp.where(ti >= ui, ret[sl], les[sl]) * NT ** (-0.5)).astype(bf16)
        return carry

    lax.fori_loop(0, NORB, products, 0)

    arrived.wait_send()
    gathered.wait_send()
    returned.wait_send()


def local(green_packed, bubble_weight, tile_owner, pairing):
    planes = green_packed.reshape(8, NT, NT)
    vmem = pl.BlockSpec(memory_space=pltpu.VMEM)
    dma = pltpu.SemaphoreType.DMA
    out = pl.pallas_call(
        kernel,
        out_shape=jax.ShapeDtypeStruct((8, NT, NT), bf16),
        in_specs=[vmem, pl.BlockSpec(memory_space=pltpu.SMEM)],
        out_specs=vmem,
        scratch_shapes=[
            pltpu.VMEM((16 * NT, HALF), f32),
            pltpu.VMEM((NDEV, 16, HALF), bf16),
            pltpu.VMEM((NDEV, 16, HALF), bf16),
            pltpu.VMEM((2, K, 8, HALF), f32),
            pltpu.VMEM((NDEV, 16, HALF), bf16),
            pltpu.VMEM((NDEV, 16, HALF), bf16),
            pltpu.VMEM((2, NDEV, 8, HALF), f32),
            pltpu.VMEM((64, 8, HALF), f32),
            pltpu.VMEM((NDEV, 16, HALF), bf16),
            pltpu.VMEM((NDEV, 16, HALF), bf16),
            pltpu.VMEM((NORB, 8, NT, NT), bf16),
            pltpu.VMEM((NORB, 8, NT, NT), bf16),
            pltpu.VMEM((NORB, 16, NT, NT), bf16),
            pltpu.VMEM((2 * NT, 16 * NT), bf16),
        ]
        + [dma] * 7,
        compiler_params=pltpu.CompilerParams(has_side_effects=True, vmem_limit_bytes=56 << 20),
        cost_estimate=pl.CostEstimate(flops=7 * 10**9, bytes_accessed=2 << 20, transcendentals=0),
    )(planes, bubble_weight)
    return out.reshape(green_packed.shape)


def solution(mesh):
    return jax.shard_map(
        local,
        mesh=mesh,
        in_specs=(P(None, "wide", "orb", None, None), P(), P(), P()),
        out_specs=P(None, "wide", "orb", None, None),
        check_vma=False,
    )
```

```python
import math

import jax
import jax.numpy as jnp
from jax import lax
from jax.experimental import pallas as pl
from jax.experimental.pallas import tpu as pltpu
from jax.sharding import PartitionSpec as P

NORB = 4
NT = 256
K = 64
HALF = 128
NDEV = 256

f32 = jnp.float32
bf16 = jnp.bfloat16

R00, R11, R10, L00, L11, L01, A00, A11, A01 = range(9)


def shear(x, h):
    lane = lax.broadcasted_iota(jnp.int32, (NT, HALF), 1)
    if h:
        x = jnp.concatenate([x[HALF:], x[:HALF]], axis=0)
    for bit in (6, 5, 4, 3):
        m = 1 << bit
        y = x.reshape(NT // (2 * m), 2, m, HALF)
        swapped = jnp.concatenate([y[:, 1:2], y[:, 0:1]], axis=1).reshape(NT, HALF)
        x = jnp.where((lane & m) != 0, swapped, x)
    lane = lax.broadcasted_iota(jnp.int32, (NT // 8, 8, HALF), 2)
    row = lax.broadcasted_iota(jnp.int32, (NT // 8, 8, HALF), 1)
    x = x.reshape(NT // 8, 8, HALF)
    for bit in (2, 1, 0):
        m = 1 << bit
        swapped = pltpu.roll(x, m, 1)
        if bit < 2:
            swapped = jnp.where((row & m) != 0, swapped, pltpu.roll(x, 8 - m, 1))
        x = jnp.where((lane & m) != 0, swapped, x)
    return x.reshape(NT, HALF)


def add(u, v):
    return (u[0] + v[0], u[1] + v[1])


def sub(u, v):
    return (u[0] - v[0], u[1] - v[1])


def times(u, cr, ci):
    return (u[0] * cr - u[1] * ci, u[0] * ci + u[1] * cr)


def turn(u, sign):
    return (-u[1], u[0]) if sign > 0 else (u[1], -u[0])


def fft4(a, b, c, d, sign):
    t0, t1, t2, t3 = add(a, c), sub(a, c), add(b, d), turn(sub(b, d), sign)
    return [add(t0, t2), add(t1, t3), sub(t0, t2), sub(t1, t3)]


def fft8(x, sign):
    even = fft4(x[0], x[2], x[4], x[6], sign)
    odd = fft4(x[1], x[3], x[5], x[7], sign)
    c = math.sqrt(0.5)
    odd = [
        odd[0],
        ((odd[1][0] - sign * odd[1][1]) * c, (sign * odd[1][0] + odd[1][1]) * c),
        turn(odd[2], sign),
        ((-odd[3][0] - sign * odd[3][1]) * c, (sign * odd[3][0] - odd[3][1]) * c),
    ]
    return [add(e, o) for e, o in zip(even, odd)] + [sub(e, o) for e, o in zip(even, odd)]


def fft64(load, store, mid, sign):
    for k2 in range(8):
        y = fft8([load(8 * k1 + k2) for k1 in range(8)], sign)
        for r1 in range(8):
            v = y[r1]
            angle = 2.0 * math.pi * k2 * r1 / 64
            cr, ci = 0.125 * math.cos(angle), sign * 0.125 * math.sin(angle)
            v = times(v, cr, ci) if k2 * r1 else (v[0] * 0.125, v[1] * 0.125)
            mid[0, r1 * 8 + k2] = v[0]
            mid[1, r1 * 8 + k2] = v[1]
    for r1 in range(8):
        y = fft8([(mid[0, r1 * 8 + k2], mid[1, r1 * 8 + k2]) for k2 in range(8)], sign)
        for r2 in range(8):
            store(r1 + 8 * r2, y[r2])


def both_parts(tile):
    x = tile.astype(f32)
    return (x[:8], x[8:])


def tile_of(v):
    return jnp.concatenate([v[0], v[1]], axis=0).astype(bf16)


def kernel(
    x_ref, w_ref, o_ref, rows, snd, rcv, mid, rg, mir, self_real, wv, snd2, rcv2, g, rhs, lhs, s1, r1, s2, r2, s3, r3, s4
):
    orb = lax.axis_index("orb")
    wide = lax.axis_index("wide")
    me = wide * NORB + orb

    def place(d):
        return (d // NORB, d % NORB)

    barrier = pltpu.get_barrier_semaphore()

    def greet(i, carry):
        pl.semaphore_signal(barrier, inc=1, device_id=place((me + i) % NDEV), device_id_type=pl.DeviceIdType.MESH)
        return carry

    lax.fori_loop(1, NDEV, greet, 0)

    def shear_plane(p, carry):
        c, b = p // 4, p % 4
        for h in range(2):
            x = x_ref[p, :, h * HALF : (h + 1) * HALF].astype(f32)
            rows[pl.ds(pl.multiple_of((c * 8 + h * 4 + b) * NT, NT), NT), :] = shear(x, h)
        return carry

    lax.fori_loop(0, 8, shear_plane, 0)

    def make_tile(e):
        snd[e] = tile_of((rows[pl.ds(e, 8, stride=NT), :], rows[pl.ds(8 * NT + e, 8, stride=NT), :]))

    def pack(i, carry):
        for n in range(4):
            make_tile(i * 4 + n)
        return carry

    lax.fori_loop(0, NDEV // 4, pack, 0)
    rcv[orb, wide] = snd[me]
    pl.semaphore_wait(barrier, NDEV - 1)

    def send(i, carry):
        step, n = i // K, i % K
        there = (wide + n) % K
        plane = (orb + step) % NORB
        d = there * NORB + plane
        pltpu.make_async_remote_copy(snd.at[d], rcv.at[orb, wide], s1.at[step], r1.at[step], device_id=(there, plane)).start()
        return carry

    lax.fori_loop(1, NDEV, send, 0)

    right, left_ = (orb + 1) % NORB, (orb + 3) % NORB
    hops = [
        pltpu.make_async_remote_copy(x_ref, g.at[orb], s2.at[0], r2.at[0], device_id=(wide, right)),
        pltpu.make_async_remote_copy(x_ref, g.at[orb], s2.at[1], r2.at[1], device_id=(wide, left_)),
    ]
    for hop in hops:
        hop.start()
    own = pltpu.make_async_copy(x_ref, g.at[orb], s4)
    own.start()

    q_of = lax.broadcasted_iota(jnp.int32, (HALF, 16), 0)
    pick = (q_of % 32 // 8 * 4 + q_of % 4 == lax.broadcasted_iota(jnp.int32, (HALF, 16), 1)).astype(bf16)
    i0 = lax.broadcasted_iota(jnp.int32, (HALF, HALF), 0)
    i1 = lax.broadcasted_iota(jnp.int32, (HALF, HALF), 1)
    same = (i0 // 32 == i1 // 32) & (i0 % 8 // 4 == i1 % 8 // 4)
    weight = w_ref[...]
    high = weight.astype(bf16)
    wide_w = []
    for part in (high, (weight - high.astype(f32)).astype(bf16)):
        z = jnp.dot(pick, part, preferred_element_type=f32).astype(bf16)
        z = lax.dot_general(z, pick, (((1,), (1,)), ((), ())), preferred_element_type=f32)
        wide_w.append(jnp.where(same, z, 0.0).astype(bf16))
    wv[...] = jnp.concatenate([wide_w[0], wide_w[1], wide_w[0]], axis=1)

    arrived = []
    for step in range(NORB):
        a = (orb + NORB - step) % NORB
        count = K - 1 if step == 0 else K
        block = rcv.at[0, pl.ds(0, count)]
        arrived.append(pltpu.make_async_remote_copy(block, block, s1.at[step], r1.at[step], device_id=(wide, orb)))
        arrived[step].wait_recv()

        def store(r, v):
            rg[r * NORB + a] = tile_of(v)

        fft64(lambda k: both_parts(rcv[a, k]), store, mid, 1)

    for hop in hops:
        hop.wait_recv()
    more = [
        pltpu.make_async_remote_copy(g.at[left_, pl.ds(0, 4)], g.at[left_, pl.ds(0, 4)], s2.at[2], r2.at[2], device_id=(wide, right)),
        pltpu.make_async_remote_copy(g.at[right, pl.ds(4, 4)], g.at[right, pl.ds(4, 4)], s2.at[3], r2.at[3], device_id=(wide, left_)),
    ]
    for hop in more:
        hop.start()

    low = me % HALF
    perm = jnp.where(i0 == (i1 ^ low), 1.0, 0.0).astype(bf16)

    def mirror_rows(i, carry):
        block = rg[pl.ds(i * 32, 32)].reshape(512, HALF)
        out = jnp.dot(block, perm, preferred_element_type=f32)
        mir[pl.ds(i * 32, 32)] = out.astype(bf16).reshape(32, 16, HALF)
        return carry

    lax.fori_loop(0, 8, mirror_rows, 0)

    swap = (lax.broadcasted_iota(jnp.int32, (8, HALF), 0) * 0 + me // HALF) == 1

    def sites(i, carry):
        prod_re, prod_im = [], []
        for n in range(4):
            r = i * 4 + n
            back = (K - r) % K
            for a in range(4):
                u = both_parts(rg[r * NORB + a])
                v = both_parts(mir[back * NORB + a])
                v = tuple(jnp.where(swap, pltpu.roll(z, 4, 0), z) for z in v)
                prod_re.append(u[0] * v[0] - u[1] * v[1])
                prod_im.append(u[0] * v[1] + u[1] * v[0])
        prod = jnp.concatenate([jnp.concatenate(prod_re, axis=0), jnp.concatenate(prod_im, axis=0)], axis=1)
        high = prod.astype(bf16)
        rest = (prod - high.astype(f32)).astype(bf16)
        bubble = jnp.dot(wv[...], jnp.concatenate([high, high, rest], axis=0), preferred_element_type=f32)
        for n in range(4):
            r = i * 4 + n
            for a in range(4):
                row = (n * 4 + a) * 8
                re, im = bubble[row : row + 8, :HALF], bubble[row : row + 8, HALF:]
                u = both_parts(rg[r * NORB + a])
                self_real[0, r * NORB + a] = u[0] * re - u[1] * im
                self_real[1, r * NORB + a] = u[0] * im + u[1] * re
        return carry

    lax.fori_loop(0, K // 4, sites, 0)

    for step in range(NORB):
        a = (orb + step) % NORB

        def store(k, v):
            snd2[k * NORB + a] = tile_of(v)

        fft64(lambda r: (self_real[0, r * NORB + a], self_real[1, r * NORB + a]), store, mid, -1)

        def send_back(n, carry):
            k = (wide + n) % K
            pltpu.make_async_remote_copy(
                snd2.at[k * NORB + a], rcv2.at[orb, wide], s3.at[step], r3.at[step], device_id=(k, a)
            ).start()
            return carry

        lax.fori_loop(1 if step == 0 else 0, K, send_back, 0)
    rcv2[orb, wide] = snd2[me]

    own.wait()
    for hop in more:
        hop.wait_recv()
    ge, gt = i0 >= i1, i0 > i1

    def operands(i, carry):
        c, bp = i // 2, i % 2
        for half in range(2):
            b = bp * 2 + half
            lanes = slice(half * HALF, (half + 1) * HALF)
            for part in range(2):
                m = pl.ds(pl.multiple_of((c * 2 + part) * HALF, HALF), HALF)
                own_g = g[c, part * 4 + b].astype(f32)
                adjoint = g[b, part * 4 + c].astype(f32).T
                if part:
                    adjoint = -adjoint
                for n in range(2):
                    blk = slice(n * HALF, (n + 1) * HALF)
                    x, y = own_g[blk, blk], adjoint[blk, blk]
                    rhs[R00 + n, bp, m, lanes] = jnp.where(ge, x, 0.0).astype(bf16)
                    rhs[L00 + n, bp, m, lanes] = jnp.where(ge, jnp.where(gt, -y, 0.0), x).astype(bf16)
                    rhs[A00 + n, bp, m, lanes] = jnp.where(gt, 0.0, y).astype(bf16)
                rhs[R10, bp, m, lanes] = own_g[HALF:, :HALF].astype(bf16)
                rhs[L01, bp, m, lanes] = own_g[:HALF, HALF:].astype(bf16)
                rhs[A01, bp, m, lanes] = adjoint[:HALF, HALF:].astype(bf16)
        return carry

    lax.fori_loop(0, 8, operands, 0)

    returned = []
    for step in range(NORB):
        count = K - 1 if step == 0 else K
        block = rcv2.at[0, pl.ds(0, count)]
        returned.append(pltpu.make_async_remote_copy(block, block, s3.at[step], r3.at[step], device_id=(wide, orb)))
        returned[step].wait_recv()
        plane = (orb + NORB - step) % NORB

        def spread(i, carry):
            for n in range(4):
                w = i * 4 + n
                e = w * NORB + plane
                re, im = both_parts(rcv2[plane, w])
                rows[pl.ds(e, 8, stride=NT), :] = re
                rows[pl.ds(8 * NT + e, 8, stride=NT), :] = im
            return carry

        lax.fori_loop(0, K // 4, spread, 0)

    def left(c, carry):
        for h in range(2):
            for part in range(2):
                x = shear(rows[pl.ds(pl.multiple_of((part * 8 + h * 4 + c) * NT, NT), NT), :], h)
                top, low_half = x[:HALF], x[HALF:]
                if h == 0:
                    placed = ((0, 0, jnp.where(ge, top, 0.0)), (0, 1, jnp.where(ge, 0.0, top)), (1, 0, low_half))
                else:
                    placed = ((0, 2, top), (1, 1, jnp.where(ge, low_half, 0.0)), (1, 2, jnp.where(ge, 0.0, low_half)))
                for t, n, z in placed:
                    same = pl.multiple_of(n * 8 * HALF + (c * 2 + part) * HALF, HALF)
                    other = pl.multiple_of(n * 8 * HALF + (c * 2 + 1 - part) * HALF, HALF)
                    lhs[t, :HALF, pl.ds(same, HALF)] = (-z if part else z).astype(bf16)
                    lhs[t, HALF:, pl.ds(other, HALF)] = z.astype(bf16)
        return carry

    lax.fori_loop(0, NORB, left, 0)

    def products(bp, carry):
        def dot(t, first, *blocks):
            z = lhs[t, :, first * 8 * HALF : (first + len(blocks)) * 8 * HALF]
            return jnp.dot(z, jnp.concatenate([rhs[n, bp] for n in blocks], axis=0), preferred_element_type=f32)

        mask = jnp.concatenate([jnp.concatenate([ge, ge], axis=0)] * 2, axis=1)
        quarters = {
            (0, 0): jnp.where(mask, dot(0, 0, R00), dot(0, 0, L00, A00)),
            (0, 1): dot(0, 0, L01, A01, A11),
            (1, 0): dot(1, 0, R00, R10),
            (1, 1): jnp.where(mask, dot(1, 1, R11), dot(1, 0, L01, L11, A11)),
        }
        for (t, u), z in quarters.items():
            z = (z * NT ** (-0.5)).astype(bf16)
            for part in range(2):
                for half in range(2):
                    o_ref[part * 4 + bp * 2 + half, t * HALF : (t + 1) * HALF, u * HALF : (u + 1) * HALF] = z[
                        part * HALF : (part + 1) * HALF, half * HALF : (half + 1) * HALF
                    ]
        return carry

    lax.fori_loop(0, 2, products, 0)

    for copy in arrived + hops + more + returned:
        copy.wait_send()


def local(green_packed, bubble_weight, tile_owner, pairing):
    planes = green_packed.reshape(8, NT, NT)
    vmem = pl.BlockSpec(memory_space=pltpu.VMEM)
    dma = pltpu.SemaphoreType.DMA
    out = pl.pallas_call(
        kernel,
        out_shape=jax.ShapeDtypeStruct((8, NT, NT), bf16),
        in_specs=[vmem, vmem],
        out_specs=vmem,
        scratch_shapes=[
            pltpu.VMEM((16 * NT, HALF), f32),
            pltpu.VMEM((NDEV, 16, HALF), bf16),
            pltpu.VMEM((NORB, K, 16, HALF), bf16),
            pltpu.VMEM((2, K, 8, HALF), f32),
            pltpu.VMEM((NDEV, 16, HALF), bf16),
            pltpu.VMEM((NDEV, 16, HALF), bf16),
            pltpu.VMEM((2, NDEV, 8, HALF), f32),
            pltpu.VMEM((HALF, 3 * HALF), bf16),
            pltpu.VMEM((NDEV, 16, HALF), bf16),
            pltpu.VMEM((NORB, K, 16, HALF), bf16),
            pltpu.VMEM((NORB, 8, NT, NT), bf16),
            pltpu.VMEM((9, 2, 8 * HALF, NT), bf16),
            pltpu.VMEM((2, NT, 24 * HALF), bf16),
        ]
        + [dma((4,))] * 6
        + [dma],
        compiler_params=pltpu.CompilerParams(has_side_effects=True, collective_id=0, vmem_limit_bytes=56 << 20),
        cost_estimate=pl.CostEstimate(flops=7 * 10**9, bytes_accessed=2 << 20, transcendentals=0),
    )(planes, bubble_weight)
    return out.reshape(green_packed.shape)


def solution(mesh):
    return jax.shard_map(
        local,
        mesh=mesh,
        in_specs=(P(None, "wide", "orb", None, None), P(), P(), P()),
        out_specs=P(None, "wide", "orb", None, None),
        check_vma=False,
    )
```

```python
import functools
import math

import jax
import jax.numpy as jnp
from jax import lax
from jax.experimental import pallas as pl
from jax.experimental.pallas import tpu as pltpu
from jax.sharding import PartitionSpec as P

NORB = 4
NT = 256
K = 64
HALF = 128
NDEV = 256
STEP = 264
ORDER = (2, 1, 3, 0)
FIRST = {0: 4}
SECOND = {4: 2}

f32 = jnp.float32
bf16 = jnp.bfloat16

R10, R00, R11, A00, L00, A01, L01, A11, L11 = range(9)


def shear(x, h):
    lane = lax.broadcasted_iota(jnp.int32, (NT, HALF), 1)
    if h:
        x = jnp.concatenate([x[HALF:], x[:HALF]], axis=0)
    for bit in (6, 5, 4, 3):
        m = 1 << bit
        y = x.reshape(NT // (2 * m), 2, m, HALF)
        swapped = jnp.concatenate([y[:, 1:2], y[:, 0:1]], axis=1).reshape(NT, HALF)
        x = jnp.where((lane & m) != 0, swapped, x)
    lane = lax.broadcasted_iota(jnp.int32, (NT // 8, 8, HALF), 2)
    row = lax.broadcasted_iota(jnp.int32, (NT // 8, 8, HALF), 1)
    x = x.reshape(NT // 8, 8, HALF)
    for bit in (2, 1, 0):
        m = 1 << bit
        swapped = pltpu.roll(x, m, 1)
        if bit < 2:
            swapped = jnp.where((row & m) != 0, swapped, pltpu.roll(x, 8 - m, 1))
        x = jnp.where((lane & m) != 0, swapped, x)
    return x.reshape(NT, HALF)


def add(u, v):
    return (u[0] + v[0], u[1] + v[1])


def sub(u, v):
    return (u[0] - v[0], u[1] - v[1])


def times(u, cr, ci):
    return (u[0] * cr - u[1] * ci, u[0] * ci + u[1] * cr)


def turn(u, sign):
    return (-u[1], u[0]) if sign > 0 else (u[1], -u[0])


def fft4(a, b, c, d, sign):
    t0, t1, t2, t3 = add(a, c), sub(a, c), add(b, d), turn(sub(b, d), sign)
    return [add(t0, t2), add(t1, t3), sub(t0, t2), sub(t1, t3)]


def fft8(x, sign):
    even = fft4(x[0], x[2], x[4], x[6], sign)
    odd = fft4(x[1], x[3], x[5], x[7], sign)
    c = math.sqrt(0.5)
    odd = [
        odd[0],
        ((odd[1][0] - sign * odd[1][1]) * c, (sign * odd[1][0] + odd[1][1]) * c),
        turn(odd[2], sign),
        ((-odd[3][0] - sign * odd[3][1]) * c, (sign * odd[3][0] - odd[3][1]) * c),
    ]
    return [add(e, o) for e, o in zip(even, odd)] + [sub(e, o) for e, o in zip(even, odd)]


def fft64(load, store, mid, sign):
    for k2 in range(8):
        y = fft8([load(8 * k1 + k2) for k1 in range(8)], sign)
        for r1 in range(8):
            v = y[r1]
            angle = 2.0 * math.pi * k2 * r1 / 64
            cr, ci = 0.125 * math.cos(angle), sign * 0.125 * math.sin(angle)
            v = times(v, cr, ci) if k2 * r1 else (v[0] * 0.125, v[1] * 0.125)
            mid[0, r1 * 8 + k2] = v[0]
            mid[1, r1 * 8 + k2] = v[1]
    for r1 in range(8):
        y = fft8([(mid[0, r1 * 8 + k2], mid[1, r1 * 8 + k2]) for k2 in range(8)], sign)
        for r2 in range(8):
            store(r1 + 8 * r2, y[r2])


def both_parts(tile):
    x = tile.astype(f32)
    return (x[:8], x[8:])


def tile_of(v):
    return jnp.concatenate([v[0], v[1]], axis=0).astype(bf16)


def kernel(
    x_ref, w_ref, o_ref, rows, snd, rcv, mid, rg, mir, self_real, wv, snd2, rcv2, g, rhs, lhs, s1, r1, s2, r2, s3, r3, s4
):
    orb = lax.axis_index("orb")
    wide = lax.axis_index("wide")
    me = wide * NORB + orb

    def place(d):
        return (d // NORB, d % NORB)

    barrier = pltpu.get_barrier_semaphore()

    def greet(i):
        pl.semaphore_signal(barrier, inc=1, device_id=place((me + i) % NDEV), device_id_type=pl.DeviceIdType.MESH)

    for i in range(249, 256):
        greet(i)

    def shear_plane(p, carry):
        for n in range(32):
            if n < 31:
                greet(p * 31 + n + 1)

        c, b = p // 4, p % 4
        for h in range(2):
            x = x_ref[p, :, h * HALF : (h + 1) * HALF].astype(f32)
            rows[pl.ds(pl.multiple_of((c * 8 + h * 4 + b) * STEP, 8), NT), :] = shear(x, h)
        return carry

    lax.fori_loop(0, 8, shear_plane, 0)

    def make_tile(e):
        snd[e] = tile_of((rows[pl.ds(e, 8, stride=STEP), :], rows[pl.ds(8 * STEP + e, 8, stride=STEP), :]))

    def pack(i, carry):
        for n in range(4):
            make_tile(i * 4 + n)
        return carry

    lax.fori_loop(0, NDEV // 4, pack, 0)
    rcv[orb, wide] = snd[me]
    pl.semaphore_wait(barrier, NDEV - 1)

    def send(step, i, carry):
        n = i % K
        there = (wide + n) % K
        plane = (orb + step) % NORB
        d = there * NORB + plane
        pltpu.make_async_remote_copy(snd.at[d], rcv.at[orb, wide], s1.at[step], r1.at[step], device_id=(there, plane)).start()
        return carry

    for step in ORDER:
        lax.fori_loop(0 if step else 1, K, functools.partial(send, step), 0)

    right, left_ = (orb + 1) % NORB, (orb + 3) % NORB
    started, halves = [], []

    def hop(source, planes, target, n):
        copy = pltpu.make_async_remote_copy(source, planes, s2.at[n], r2.at[n], device_id=(wide, target))
        copy.start()
        return copy

    def gather(when):
        for _ in range(FIRST.get(when, 0)):
            n = len(started)
            up, down = pl.ds(2 * n, 2), pl.ds(6 - 2 * n, 2)
            started.append((hop(x_ref.at[up], g.at[orb, up], right, n), hop(x_ref.at[down], g.at[orb, down], left_, 4 + n)))
        for _ in range(SECOND.get(when, 0)):
            n = len(halves)
            up, down = pl.ds(2 * n, 2), pl.ds(6 - 2 * n, 2)
            for copy in started[n]:
                copy.wait_recv()
            halves.append((hop(g.at[left_, up], g.at[left_, up], right, 8 + n), hop(g.at[right, down], g.at[right, down], left_, 10 + n)))

    gather(0)
    own = pltpu.make_async_copy(x_ref, g.at[orb], s4)
    own.start()

    q_of = lax.broadcasted_iota(jnp.int32, (HALF, 16), 0)
    pick = (q_of % 32 // 8 * 4 + q_of % 4 == lax.broadcasted_iota(jnp.int32, (HALF, 16), 1)).astype(bf16)
    i0 = lax.broadcasted_iota(jnp.int32, (HALF, HALF), 0)
    i1 = lax.broadcasted_iota(jnp.int32, (HALF, HALF), 1)
    same = (i0 // 32 == i1 // 32) & (i0 % 8 // 4 == i1 % 8 // 4)
    weight = w_ref[...]
    high = weight.astype(bf16)
    wide_w = []
    for part in (high, (weight - high.astype(f32)).astype(bf16)):
        z = jnp.dot(pick, part, preferred_element_type=f32).astype(bf16)
        z = lax.dot_general(z, pick, (((1,), (1,)), ((), ())), preferred_element_type=f32)
        wide_w.append(jnp.where(same, z, 0.0).astype(bf16))
    wv[...] = jnp.concatenate([wide_w[0], wide_w[1], wide_w[0]], axis=1)

    low = me % HALF
    perm = jnp.where(i0 == (i1 ^ low), 1.0, 0.0).astype(bf16)

    arrived = []
    for step in ORDER:
        a = (orb + NORB - step) % NORB
        count = K - 1 if step == 0 else K
        block = rcv.at[0, pl.ds(0, count)]
        arrived.append(pltpu.make_async_remote_copy(block, block, s1.at[step], r1.at[step], device_id=(wide, orb)))
        arrived[-1].wait_recv()

        def store(r, v):
            rg[a, r] = tile_of(v)

        fft64(lambda k: both_parts(rcv[a, k]), store, mid, 1)
        gather(len(arrived))
        for n in range(2):
            block = rg[a, n * 32 : (n + 1) * 32].reshape(32 * 16, HALF)
            out = jnp.dot(block, perm, preferred_element_type=f32)
            mir[a, n * 32 : (n + 1) * 32] = out.astype(bf16).reshape(32, 16, HALF)

    swap = (lax.broadcasted_iota(jnp.int32, (8, HALF), 0) * 0 + me // HALF) == 1

    def four_sites(first):
        prod_re, prod_im, owns = [], [], []
        for n in range(4):
            r = first + n
            back = (K - r) % K
            for a in range(4):
                u = both_parts(rg[a, r])
                v = both_parts(mir[a, back])
                v = tuple(jnp.where(swap, pltpu.roll(z, 4, 0), z) for z in v)
                prod_re.append(u[0] * v[0] - u[1] * v[1])
                prod_im.append(u[0] * v[1] + u[1] * v[0])
        prod = jnp.concatenate([jnp.concatenate(prod_re, axis=0), jnp.concatenate(prod_im, axis=0)], axis=1)
        high = prod.astype(bf16)
        rest = (prod - high.astype(f32)).astype(bf16)
        return jnp.dot(wv[...], jnp.concatenate([high, high, rest], axis=0), preferred_element_type=f32)

    def sites(i, carry):
        bubbles = [four_sites(i * 16 + m * 4) for m in range(4)]
        for m in range(4):
            for n in range(4):
                r = i * 16 + m * 4 + n
                for a in range(4):
                    row = (n * 4 + a) * 8
                    re, im = bubbles[m][row : row + 8, :HALF], bubbles[m][row : row + 8, HALF:]
                    u = both_parts(rg[a, r])
                    self_real[0, r * NORB + a] = u[0] * re - u[1] * im
                    self_real[1, r * NORB + a] = u[0] * im + u[1] * re
        return carry

    lax.fori_loop(0, K // 16, sites, 0)

    gather(5)

    for turn_n, step in enumerate(ORDER):
        a = (orb + step) % NORB

        def store(k, v):
            snd2[k * NORB + a] = tile_of(v)

        fft64(lambda r: (self_real[0, r * NORB + a], self_real[1, r * NORB + a]), store, mid, -1)

        def send_back(n, carry):
            k = (wide + n) % K
            pltpu.make_async_remote_copy(
                snd2.at[k * NORB + a], rcv2.at[orb, wide], s3.at[step], r3.at[step], device_id=(k, a)
            ).start()
            return carry

        lax.fori_loop(1 if step == 0 else 0, K, send_back, 0)
        gather(6 + turn_n)
    rcv2[orb, wide] = snd2[me]

    own.wait()
    for copy in sum(started[2:] + halves, ()):
        copy.wait_recv()
    ge, gt = i0 >= i1, i0 > i1

    def operands(i, carry):
        c, bp = i // 2, i % 2
        for half in range(2):
            b = bp * 2 + half
            lanes = slice(half * HALF, (half + 1) * HALF)
            for part in range(2):
                def m(block):
                    return pl.ds(pl.multiple_of(block * 8 * HALF + (c * 2 + part) * HALF, HALF), HALF)

                own_g = g[c, part * 4 + b].astype(f32)
                adjoint = g[b, part * 4 + c].astype(f32).T
                if part:
                    adjoint = -adjoint
                for n in range(2):
                    blk = slice(n * HALF, (n + 1) * HALF)
                    x, y = own_g[blk, blk], adjoint[blk, blk]
                    rhs[bp, m((R00, R11)[n]), lanes] = jnp.where(ge, x, 0.0).astype(bf16)
                    rhs[bp, m((L00, L11)[n]), lanes] = jnp.where(ge, jnp.where(gt, -y, 0.0), x).astype(bf16)
                    rhs[bp, m((A00, A11)[n]), lanes] = jnp.where(gt, 0.0, y).astype(bf16)
                rhs[bp, m(R10), lanes] = own_g[HALF:, :HALF].astype(bf16)
                rhs[bp, m(L01), lanes] = own_g[:HALF, HALF:].astype(bf16)
                rhs[bp, m(A01), lanes] = adjoint[:HALF, HALF:].astype(bf16)
        return carry

    lax.fori_loop(0, 8, operands, 0)

    returned = []
    for step in ORDER:
        count = K - 1 if step == 0 else K
        block = rcv2.at[0, pl.ds(0, count)]
        returned.append(pltpu.make_async_remote_copy(block, block, s3.at[step], r3.at[step], device_id=(wide, orb)))
        returned[-1].wait_recv()
        plane = (orb + NORB - step) % NORB

        def spread(i, carry):
            for n in range(4):
                w = i * 4 + n
                e = w * NORB + plane
                re, im = both_parts(rcv2[plane, w])
                rows[pl.ds(e, 8, stride=STEP), :] = re
                rows[pl.ds(8 * STEP + e, 8, stride=STEP), :] = im
            return carry

        lax.fori_loop(0, K // 4, spread, 0)

    def left(c, carry):
        for h in range(2):
            for part in range(2):
                x = shear(rows[pl.ds(pl.multiple_of((part * 8 + h * 4 + c) * STEP, 8), NT), :], h)
                top, low_half = x[:HALF], x[HALF:]
                if h == 0:
                    placed = ((0, 1, jnp.where(ge, top, 0.0)), (0, 0, jnp.where(ge, 0.0, top)), (1, 0, low_half), (1, 3, low_half))
                else:
                    placed = ((0, 2, top), (1, 2, jnp.where(ge, low_half, 0.0)), (1, 1, jnp.where(ge, 0.0, low_half)))
                for t, n, z in placed:
                    same = pl.multiple_of(n * 8 * HALF + (c * 2 + part) * HALF, HALF)
                    other = pl.multiple_of(n * 8 * HALF + (c * 2 + 1 - part) * HALF, HALF)
                    lhs[t, :HALF, pl.ds(same, HALF)] = (-z if part else z).astype(bf16)
                    lhs[t, HALF:, pl.ds(other, HALF)] = z.astype(bf16)
        return carry

    lax.fori_loop(0, NORB, left, 0)

    def products(bp, carry):
        def dot(t, first, block, count=1):
            z = lhs[t, :, first * 8 * HALF : (first + count) * 8 * HALF]
            return jnp.dot(z, rhs[bp, block * 8 * HALF : (block + count) * 8 * HALF], preferred_element_type=f32)

        mask = jnp.concatenate([jnp.concatenate([ge, ge], axis=0)] * 2, axis=1)
        quarters = {
            (0, 0): jnp.where(mask, dot(0, 1, R00), dot(0, 0, A00, 2)),
            (0, 1): dot(0, 0, A01, 3),
            (1, 0): dot(1, 2, R10, 2),
            (1, 1): jnp.where(mask, dot(1, 2, R11), dot(1, 0, L01, 3)),
        }
        for (t, u), z in quarters.items():
            z = z.astype(bf16)
            for part in range(2):
                for half in range(2):
                    o_ref[part * 4 + bp * 2 + half, t * HALF : (t + 1) * HALF, u * HALF : (u + 1) * HALF] = z[
                        part * HALF : (part + 1) * HALF, half * HALF : (half + 1) * HALF
                    ]
        return carry

    lax.fori_loop(0, 2, products, 0)

    for copy in arrived + list(sum(started + halves, ())) + returned:
        copy.wait_send()


def local(green_packed, bubble_weight, tile_owner, pairing):
    planes = green_packed.reshape(8, NT, NT)
    vmem = pl.BlockSpec(memory_space=pltpu.VMEM)
    dma = pltpu.SemaphoreType.DMA
    out = pl.pallas_call(
        kernel,
        out_shape=jax.ShapeDtypeStruct((8, NT, NT), bf16),
        in_specs=[vmem, vmem],
        out_specs=vmem,
        scratch_shapes=[
            pltpu.VMEM((16 * STEP, HALF), f32),
            pltpu.VMEM((NDEV, 16, HALF), bf16),
            pltpu.VMEM((NORB, K, 16, HALF), bf16),
            pltpu.VMEM((2, K, 8, HALF), f32),
            pltpu.VMEM((NORB, K, 16, HALF), bf16),
            pltpu.VMEM((NORB, K, 16, HALF), bf16),
            pltpu.VMEM((2, NDEV, 8, HALF), f32),
            pltpu.VMEM((HALF, 3 * HALF), bf16),
            pltpu.VMEM((NDEV, 16, HALF), bf16),
            pltpu.VMEM((NORB, K, 16, HALF), bf16),
            pltpu.VMEM((NORB, 8, NT, NT), bf16),
            pltpu.VMEM((2, 72 * HALF, NT), bf16),
            pltpu.VMEM((2, NT, 32 * HALF), bf16),
        ]
        + [dma((4,))] * 2
        + [dma((12,))] * 2
        + [dma((4,))] * 2
        + [dma],
        compiler_params=pltpu.CompilerParams(has_side_effects=True, collective_id=0, vmem_limit_bytes=56 << 20),
        cost_estimate=pl.CostEstimate(flops=7 * 10**9, bytes_accessed=2 << 20, transcendentals=0),
    )(planes, bubble_weight)
    return out.reshape(green_packed.shape) * jnp.asarray(NT ** (-0.5), bf16)


def solution(mesh):
    return jax.shard_map(
        local,
        mesh=mesh,
        in_specs=(P(None, "wide", "orb", None, None), P(), P(), P()),
        out_specs=P(None, "wide", "orb", None, None),
        check_vma=False,
    )
```

```python
import functools
import math

import jax
import jax.numpy as jnp
from jax import lax
from jax.experimental import pallas as pl
from jax.experimental.pallas import tpu as pltpu
from jax.sharding import PartitionSpec as P

NORB = 4
NT = 256
K = 64
HALF = 128
NDEV = 256
STEP = 264
ORDER = (2, 1, 3, 0)
FIRST = {0: 4}
SECOND = {4: 2}

f32 = jnp.float32
bf16 = jnp.bfloat16

R10, R00, R11, A00, L00, A01, L01, A11, L11 = range(9)


def shear(x, h):
    lane = lax.broadcasted_iota(jnp.int32, (NT, HALF), 1)
    if h:
        x = jnp.concatenate([x[HALF:], x[:HALF]], axis=0)
    for bit in (6, 5, 4, 3):
        m = 1 << bit
        y = x.reshape(NT // (2 * m), 2, m, HALF)
        swapped = jnp.concatenate([y[:, 1:2], y[:, 0:1]], axis=1).reshape(NT, HALF)
        x = jnp.where((lane & m) != 0, swapped, x)
    lane = lax.broadcasted_iota(jnp.int32, (NT // 8, 8, HALF), 2)
    row = lax.broadcasted_iota(jnp.int32, (NT // 8, 8, HALF), 1)
    x = x.reshape(NT // 8, 8, HALF)
    for bit in (2, 1, 0):
        m = 1 << bit
        swapped = pltpu.roll(x, m, 1)
        if bit < 2:
            swapped = jnp.where((row & m) != 0, swapped, pltpu.roll(x, 8 - m, 1))
        x = jnp.where((lane & m) != 0, swapped, x)
    return x.reshape(NT, HALF)


def add(u, v):
    return (u[0] + v[0], u[1] + v[1])


def sub(u, v):
    return (u[0] - v[0], u[1] - v[1])


def times(u, cr, ci):
    return (u[0] * cr - u[1] * ci, u[0] * ci + u[1] * cr)


def turn(u, sign):
    return (-u[1], u[0]) if sign > 0 else (u[1], -u[0])


def fft4(a, b, c, d, sign):
    t0, t1, t2, t3 = add(a, c), sub(a, c), add(b, d), turn(sub(b, d), sign)
    return [add(t0, t2), add(t1, t3), sub(t0, t2), sub(t1, t3)]


def fft8(x, sign):
    even = fft4(x[0], x[2], x[4], x[6], sign)
    odd = fft4(x[1], x[3], x[5], x[7], sign)
    c = math.sqrt(0.5)
    odd = [
        odd[0],
        ((odd[1][0] - sign * odd[1][1]) * c, (sign * odd[1][0] + odd[1][1]) * c),
        turn(odd[2], sign),
        ((-odd[3][0] - sign * odd[3][1]) * c, (sign * odd[3][0] - odd[3][1]) * c),
    ]
    return [add(e, o) for e, o in zip(even, odd)] + [sub(e, o) for e, o in zip(even, odd)]


def fft64(load, store, mid, sign):
    for k2 in range(8):
        y = fft8([load(8 * k1 + k2) for k1 in range(8)], sign)
        for r1 in range(8):
            v = y[r1]
            angle = 2.0 * math.pi * k2 * r1 / 64
            cr, ci = 0.125 * math.cos(angle), sign * 0.125 * math.sin(angle)
            v = times(v, cr, ci) if k2 * r1 else (v[0] * 0.125, v[1] * 0.125)
            mid[0, r1 * 8 + k2] = v[0]
            mid[1, r1 * 8 + k2] = v[1]
    for r1 in range(8):
        y = fft8([(mid[0, r1 * 8 + k2], mid[1, r1 * 8 + k2]) for k2 in range(8)], sign)
        for r2 in range(8):
            store(r1 + 8 * r2, y[r2])


def both_parts(tile):
    x = tile.astype(f32)
    return (x[:8], x[8:])


def tile_of(v):
    return jnp.concatenate([v[0], v[1]], axis=0).astype(bf16)


def kernel(
    x_ref, w_ref, o_ref, rows, snd, rcv, mid, rg, mir, self_real, wv, snd2, rcv2, g, rhs, lhs, s1, r1, s2, r2, s3, r3, s4
):
    orb = lax.axis_index("orb")
    wide = lax.axis_index("wide")
    me = wide * NORB + orb

    def place(d):
        return (d // NORB, d % NORB)

    barrier = pltpu.get_barrier_semaphore()

    def greet(i):
        pl.semaphore_signal(barrier, inc=1, device_id=place((me + i) % NDEV), device_id_type=pl.DeviceIdType.MESH)

    for i in range(249, 256):
        greet(i)

    def shear_plane(p, carry):
        for n in range(32):
            if n < 31:
                greet(p * 31 + n + 1)

        c, b = p // 4, p % 4
        for h in range(2):
            x = x_ref[p, :, h * HALF : (h + 1) * HALF].astype(f32)
            rows[pl.ds(pl.multiple_of((c * 8 + h * 4 + b) * STEP, 8), NT), :] = shear(x, h)
        return carry

    lax.fori_loop(0, 8, shear_plane, 0)

    def make_tile(e):
        snd[e] = tile_of((rows[pl.ds(e, 8, stride=STEP), :], rows[pl.ds(8 * STEP + e, 8, stride=STEP), :]))

    def pack(i, carry):
        for n in range(4):
            make_tile(i * 4 + n)
        return carry

    lax.fori_loop(0, NDEV // 4, pack, 0)
    rcv[orb, wide] = snd[me]
    pl.semaphore_wait(barrier, NDEV - 1)

    def send(step, i, carry):
        n = i % K
        there = (wide + n) % K
        plane = (orb + step) % NORB
        d = there * NORB + plane
        pltpu.make_async_remote_copy(snd.at[d], rcv.at[orb, wide], s1.at[step], r1.at[step], device_id=(there, plane)).start()
        return carry

    for step in ORDER:
        lax.fori_loop(0 if step else 1, K, functools.partial(send, step), 0)

    right, left_ = (orb + 1) % NORB, (orb + 3) % NORB
    started, halves = [], []

    def hop(source, planes, target, n):
        copy = pltpu.make_async_remote_copy(source, planes, s2.at[n], r2.at[n], device_id=(wide, target))
        copy.start()
        return copy

    def gather(when):
        for _ in range(FIRST.get(when, 0)):
            n = len(started)
            up, down = pl.ds(2 * n, 2), pl.ds(6 - 2 * n, 2)
            started.append((hop(x_ref.at[up], g.at[orb, up], right, n), hop(x_ref.at[down], g.at[orb, down], left_, 4 + n)))
        for _ in range(SECOND.get(when, 0)):
            n = len(halves)
            up, down = pl.ds(2 * n, 2), pl.ds(6 - 2 * n, 2)
            for copy in started[n]:
                copy.wait_recv()
            halves.append((hop(g.at[left_, up], g.at[left_, up], right, 8 + n), hop(g.at[right, down], g.at[right, down], left_, 10 + n)))

    gather(0)
    own = pltpu.make_async_copy(x_ref, g.at[orb], s4)
    own.start()

    q_of = lax.broadcasted_iota(jnp.int32, (HALF, 16), 0)
    pick = (q_of % 32 // 8 * 4 + q_of % 4 == lax.broadcasted_iota(jnp.int32, (HALF, 16), 1)).astype(bf16)
    i0 = lax.broadcasted_iota(jnp.int32, (HALF, HALF), 0)
    i1 = lax.broadcasted_iota(jnp.int32, (HALF, HALF), 1)
    same = (i0 // 32 == i1 // 32) & (i0 % 8 // 4 == i1 % 8 // 4)
    weight = w_ref[...]
    high = weight.astype(bf16)
    wide_w = []
    for part in (high, (weight - high.astype(f32)).astype(bf16)):
        z = jnp.dot(pick, part, preferred_element_type=f32).astype(bf16)
        z = lax.dot_general(z, pick, (((1,), (1,)), ((), ())), preferred_element_type=f32)
        wide_w.append(jnp.where(same, z, 0.0).astype(bf16))
    wv[...] = jnp.concatenate([wide_w[0], wide_w[1], wide_w[0]], axis=1)

    low = me % HALF
    perm = jnp.where(i0 == (i1 ^ low), 1.0, 0.0).astype(bf16)

    arrived = []
    for step in ORDER:
        a = (orb + NORB - step) % NORB
        count = K - 1 if step == 0 else K
        block = rcv.at[0, pl.ds(0, count)]
        arrived.append(pltpu.make_async_remote_copy(block, block, s1.at[step], r1.at[step], device_id=(wide, orb)))
        arrived[-1].wait_recv()

        def store(r, v):
            rg[a, r] = tile_of(v)

        fft64(lambda k: both_parts(rcv[a, k]), store, mid, 1)
        gather(len(arrived))
        for n in range(2):
            block = rg[a, n * 32 : (n + 1) * 32].reshape(32 * 16, HALF)
            out = jnp.dot(block, perm, preferred_element_type=f32)
            mir[a, n * 32 : (n + 1) * 32] = out.astype(bf16).reshape(32, 16, HALF)

    swap = (lax.broadcasted_iota(jnp.int32, (8, HALF), 0) * 0 + me // HALF) == 1

    def four_sites(first):
        prod_re, prod_im, owns = [], [], []
        for n in range(4):
            r = first + n
            back = (K - r) % K
            for a in range(4):
                u = both_parts(rg[a, r])
                v = both_parts(mir[a, back])
                v = tuple(jnp.where(swap, pltpu.roll(z, 4, 0), z) for z in v)
                prod_re.append(u[0] * v[0] - u[1] * v[1])
                prod_im.append(u[0] * v[1] + u[1] * v[0])
        prod = jnp.concatenate([jnp.concatenate(prod_re, axis=0), jnp.concatenate(prod_im, axis=0)], axis=1)
        high = prod.astype(bf16)
        rest = (prod - high.astype(f32)).astype(bf16)
        return jnp.dot(wv[...], jnp.concatenate([high, high, rest], axis=0), preferred_element_type=f32)

    def sites(i, carry):
        bubbles = [four_sites(i * 16 + m * 4) for m in range(4)]
        for m in range(4):
            for n in range(4):
                r = i * 16 + m * 4 + n
                for a in range(4):
                    row = (n * 4 + a) * 8
                    re, im = bubbles[m][row : row + 8, :HALF], bubbles[m][row : row + 8, HALF:]
                    u = both_parts(rg[a, r])
                    self_real[0, r * NORB + a] = u[0] * re - u[1] * im
                    self_real[1, r * NORB + a] = u[0] * im + u[1] * re
        return carry

    lax.fori_loop(0, K // 16, sites, 0)

    gather(5)

    for turn_n, step in enumerate(ORDER):
        a = (orb + step) % NORB

        def store(k, v):
            snd2[k * NORB + a] = tile_of(v)

        fft64(lambda r: (self_real[0, r * NORB + a], self_real[1, r * NORB + a]), store, mid, -1)

        def send_back(n, carry):
            k = (wide + n) % K
            pltpu.make_async_remote_copy(
                snd2.at[k * NORB + a], rcv2.at[orb, wide], s3.at[step], r3.at[step], device_id=(k, a)
            ).start()
            return carry

        lax.fori_loop(1 if step == 0 else 0, K, send_back, 0)
        gather(6 + turn_n)
    rcv2[orb, wide] = snd2[me]

    own.wait()
    for copy in sum(started[2:] + halves, ()):
        copy.wait_recv()
    ge, gt = i0 >= i1, i0 > i1

    def operands(i, carry):
        c, bp = i // 2, i % 2
        for half in range(2):
            b = bp * 2 + half
            lanes = slice(half * HALF, (half + 1) * HALF)
            for part in range(2):
                def m(block):
                    return pl.ds(pl.multiple_of(block * 8 * HALF + (c * 2 + part) * HALF, HALF), HALF)

                own_g = g[c, part * 4 + b].astype(f32)
                adjoint = g[b, part * 4 + c].astype(f32).T
                if part:
                    adjoint = -adjoint
                for n in range(2):
                    blk = slice(n * HALF, (n + 1) * HALF)
                    x, y = own_g[blk, blk], adjoint[blk, blk]
                    rhs[bp, m((R00, R11)[n]), lanes] = jnp.where(ge, x, 0.0).astype(bf16)
                    rhs[bp, m((L00, L11)[n]), lanes] = jnp.where(ge, jnp.where(gt, -y, 0.0), x).astype(bf16)
                    rhs[bp, m((A00, A11)[n]), lanes] = jnp.where(gt, 0.0, y).astype(bf16)
                rhs[bp, m(R10), lanes] = own_g[HALF:, :HALF].astype(bf16)
                rhs[bp, m(L01), lanes] = own_g[:HALF, HALF:].astype(bf16)
                rhs[bp, m(A01), lanes] = adjoint[:HALF, HALF:].astype(bf16)
        return carry

    lax.fori_loop(0, 8, operands, 0)

    returned = []
    for step in ORDER:
        count = K - 1 if step == 0 else K
        block = rcv2.at[0, pl.ds(0, count)]
        returned.append(pltpu.make_async_remote_copy(block, block, s3.at[step], r3.at[step], device_id=(wide, orb)))
        returned[-1].wait_recv()
        plane = (orb + NORB - step) % NORB

        def spread(i, carry):
            for n in range(4):
                w = i * 4 + n
                e = w * NORB + plane
                re, im = both_parts(rcv2[plane, w])
                rows[pl.ds(e, 8, stride=STEP), :] = re
                rows[pl.ds(8 * STEP + e, 8, stride=STEP), :] = im
            return carry

        lax.fori_loop(0, K // 4, spread, 0)

    def left(c, carry):
        for h in range(2):
            for part in range(2):
                x = shear(rows[pl.ds(pl.multiple_of((part * 8 + h * 4 + c) * STEP, 8), NT), :], h)
                top, low_half = x[:HALF], x[HALF:]
                if h == 0:
                    placed = ((0, 1, jnp.where(ge, top, 0.0)), (0, 0, jnp.where(ge, 0.0, top)), (1, 0, low_half), (1, 3, low_half))
                else:
                    placed = ((0, 2, top), (1, 2, jnp.where(ge, low_half, 0.0)), (1, 1, jnp.where(ge, 0.0, low_half)))
                for t, n, z in placed:
                    same = pl.multiple_of(n * 8 * HALF + (c * 2 + part) * HALF, HALF)
                    other = pl.multiple_of(n * 8 * HALF + (c * 2 + 1 - part) * HALF, HALF)
                    lhs[t, :HALF, pl.ds(same, HALF)] = (-z if part else z).astype(bf16)
                    lhs[t, HALF:, pl.ds(other, HALF)] = z.astype(bf16)
        return carry

    lax.fori_loop(0, NORB, left, 0)

    def products(bp, carry):
        def dot(t, first, block, count=1):
            z = lhs[t, :, first * 8 * HALF : (first + count) * 8 * HALF]
            return jnp.dot(z, rhs[bp, block * 8 * HALF : (block + count) * 8 * HALF], preferred_element_type=f32)

        mask = jnp.concatenate([jnp.concatenate([ge, ge], axis=0)] * 2, axis=1)
        quarters = {
            (0, 0): jnp.where(mask, dot(0, 1, R00), dot(0, 0, A00, 2)),
            (0, 1): dot(0, 0, A01, 3),
            (1, 0): dot(1, 2, R10, 2),
            (1, 1): jnp.where(mask, dot(1, 2, R11), dot(1, 0, L01, 3)),
        }
        for (t, u), z in quarters.items():
            z = z.astype(bf16)
            for part in range(2):
                for half in range(2):
                    o_ref[part * 4 + bp * 2 + half, t * HALF : (t + 1) * HALF, u * HALF : (u + 1) * HALF] = z[
                        part * HALF : (part + 1) * HALF, half * HALF : (half + 1) * HALF
                    ]
        return carry

    lax.fori_loop(0, 2, products, 0)

    for copy in arrived + list(sum(started + halves, ())) + returned:
        copy.wait_send()


def local(green_packed, bubble_weight, tile_owner, pairing):
    planes = green_packed.reshape(8, NT, NT)
    vmem = pl.BlockSpec(memory_space=pltpu.VMEM)
    dma = pltpu.SemaphoreType.DMA
    out = pl.pallas_call(
        kernel,
        out_shape=jax.ShapeDtypeStruct((8, NT, NT), bf16),
        in_specs=[vmem, vmem],
        out_specs=vmem,
        scratch_shapes=[
            pltpu.VMEM((16 * STEP, HALF), f32),
            pltpu.VMEM((NDEV, 16, HALF), bf16),
            pltpu.VMEM((NORB, K, 16, HALF), bf16),
            pltpu.VMEM((2, K, 8, HALF), f32),
            pltpu.VMEM((NORB, K, 16, HALF), bf16),
            pltpu.VMEM((NORB, K, 16, HALF), bf16),
            pltpu.VMEM((2, NDEV, 8, HALF), f32),
            pltpu.VMEM((HALF, 3 * HALF), bf16),
            pltpu.VMEM((NDEV, 16, HALF), bf16),
            pltpu.VMEM((NORB, K, 16, HALF), bf16),
            pltpu.VMEM((NORB, 8, NT, NT), bf16),
            pltpu.VMEM((2, 72 * HALF, NT), bf16),
            pltpu.VMEM((2, NT, 32 * HALF), bf16),
        ]
        + [dma((4,))] * 2
        + [dma((12,))] * 2
        + [dma((4,))] * 2
        + [dma],
        compiler_params=pltpu.CompilerParams(has_side_effects=True, collective_id=0, vmem_limit_bytes=38 << 20),
        cost_estimate=pl.CostEstimate(flops=7 * 10**9, bytes_accessed=2 << 20, transcendentals=0),
    )(planes, bubble_weight)
    return out.reshape(green_packed.shape) * jnp.asarray(NT ** (-0.5), bf16)


def solution(mesh):
    return jax.shard_map(
        local,
        mesh=mesh,
        in_specs=(P(None, "wide", "orb", None, None), P(), P(), P()),
        out_specs=P(None, "wide", "orb", None, None),
        check_vma=False,
    )
```

```python
import functools
import math

import jax
import jax.numpy as jnp
from jax import lax
from jax.experimental import pallas as pl
from jax.experimental.pallas import tpu as pltpu
from jax.sharding import PartitionSpec as P

NORB = 4
NT = 256
K = 64
HALF = 128
NDEV = 256
STEP = 264
ORDER = (2, 1, 3, 0)
FIRST = {0: 4}
SECOND = {4: 2}

f32 = jnp.float32
bf16 = jnp.bfloat16

R10, R00, R11, A00, L00, A01, L01, A11, L11 = range(9)


def shear(x, h):
    lane = lax.broadcasted_iota(jnp.int32, (NT, HALF), 1)
    if h:
        x = jnp.concatenate([x[HALF:], x[:HALF]], axis=0)
    for bit in (6, 5, 4, 3):
        m = 1 << bit
        y = x.reshape(NT // (2 * m), 2, m, HALF)
        swapped = jnp.concatenate([y[:, 1:2], y[:, 0:1]], axis=1).reshape(NT, HALF)
        x = jnp.where((lane & m) != 0, swapped, x)
    lane = lax.broadcasted_iota(jnp.int32, (NT // 8, 8, HALF), 2)
    row = lax.broadcasted_iota(jnp.int32, (NT // 8, 8, HALF), 1)
    x = x.reshape(NT // 8, 8, HALF)
    for bit in (2, 1, 0):
        m = 1 << bit
        swapped = pltpu.roll(x, m, 1)
        if bit < 2:
            swapped = jnp.where((row & m) != 0, swapped, pltpu.roll(x, 8 - m, 1))
        x = jnp.where((lane & m) != 0, swapped, x)
    return x.reshape(NT, HALF)


def add(u, v):
    return (u[0] + v[0], u[1] + v[1])


def sub(u, v):
    return (u[0] - v[0], u[1] - v[1])


def times(u, cr, ci):
    return (u[0] * cr - u[1] * ci, u[0] * ci + u[1] * cr)


def turn(u, sign):
    return (-u[1], u[0]) if sign > 0 else (u[1], -u[0])


def fft4(a, b, c, d, sign):
    t0, t1, t2, t3 = add(a, c), sub(a, c), add(b, d), turn(sub(b, d), sign)
    return [add(t0, t2), add(t1, t3), sub(t0, t2), sub(t1, t3)]


def fft8(x, sign):
    even = fft4(x[0], x[2], x[4], x[6], sign)
    odd = fft4(x[1], x[3], x[5], x[7], sign)
    c = math.sqrt(0.5)
    odd = [
        odd[0],
        ((odd[1][0] - sign * odd[1][1]) * c, (sign * odd[1][0] + odd[1][1]) * c),
        turn(odd[2], sign),
        ((-odd[3][0] - sign * odd[3][1]) * c, (sign * odd[3][0] - odd[3][1]) * c),
    ]
    return [add(e, o) for e, o in zip(even, odd)] + [sub(e, o) for e, o in zip(even, odd)]


def fft64(load, store, mid, sign):
    for k2 in range(8):
        y = fft8([load(8 * k1 + k2) for k1 in range(8)], sign)
        for r1 in range(8):
            v = y[r1]
            angle = 2.0 * math.pi * k2 * r1 / 64
            cr, ci = 0.125 * math.cos(angle), sign * 0.125 * math.sin(angle)
            v = times(v, cr, ci) if k2 * r1 else (v[0] * 0.125, v[1] * 0.125)
            mid[0, r1 * 8 + k2] = v[0]
            mid[1, r1 * 8 + k2] = v[1]
    for r1 in range(8):
        y = fft8([(mid[0, r1 * 8 + k2], mid[1, r1 * 8 + k2]) for k2 in range(8)], sign)
        for r2 in range(8):
            store(r1 + 8 * r2, y[r2])


def both_parts(tile):
    x = tile.astype(f32)
    return (x[:8], x[8:])


def tile_of(v):
    return jnp.concatenate([v[0], v[1]], axis=0).astype(bf16)


def kernel(
    x_ref, w_ref, o_ref, rows, snd, rcv, mid, rg, mir, self_real, wv, snd2, rcv2, g, rhs, lhs, s1, r1, s2, r2, s3, r3, s4
):
    orb = lax.axis_index("orb")
    wide = lax.axis_index("wide")
    me = wide * NORB + orb

    def place(d):
        return (d // NORB, d % NORB)

    barrier = pltpu.get_barrier_semaphore()
    planes = [lax.rem(orb + step, NORB) for step in range(NORB)]

    def shear_plane(p, carry):
        for n in range(8):
            there = lax.rem(wide + p * 8 + n, K)
            for step in range(NORB):

                def greet(there=there, step=step):
                    device = (there, planes[step])
                    pl.semaphore_signal(barrier, inc=1, device_id=device, device_id_type=pl.DeviceIdType.MESH)

                if n or step:
                    greet()
                else:
                    pl.when(p > 0)(greet)

        c, b = p // 4, p % 4
        for h in range(2):
            x = x_ref[p, :, h * HALF : (h + 1) * HALF].astype(f32)
            rows[pl.ds(pl.multiple_of((c * 8 + h * 4 + b) * STEP, 8), NT), :] = shear(x, h)
        return carry

    lax.fori_loop(0, 8, shear_plane, 0)

    def make_tile(e):
        snd[e] = tile_of((rows[pl.ds(e, 8, stride=STEP), :], rows[pl.ds(8 * STEP + e, 8, stride=STEP), :]))

    def pack(i, carry):
        for n in range(4):
            make_tile(i * 4 + n)
        return carry

    lax.fori_loop(0, NDEV // 4, pack, 0)
    rcv[orb, wide] = snd[me]
    pl.semaphore_wait(barrier, NDEV - 1)

    def send(step, i, carry):
        there = lax.rem(wide + i, K)
        plane = planes[step]
        d = there * NORB + plane
        pltpu.make_async_remote_copy(snd.at[d], rcv.at[orb, wide], s1.at[step], r1.at[step], device_id=(there, plane)).start()
        return carry

    for step in ORDER:
        lax.fori_loop(0 if step else 1, K, functools.partial(send, step), 0)

    right, left_ = (orb + 1) % NORB, (orb + 3) % NORB
    started, halves = [], []

    def hop(source, planes, target, n):
        copy = pltpu.make_async_remote_copy(source, planes, s2.at[n], r2.at[n], device_id=(wide, target))
        copy.start()
        return copy

    def gather(when):
        for _ in range(FIRST.get(when, 0)):
            n = len(started)
            up, down = pl.ds(2 * n, 2), pl.ds(6 - 2 * n, 2)
            started.append((hop(x_ref.at[up], g.at[orb, up], right, n), hop(x_ref.at[down], g.at[orb, down], left_, 4 + n)))
        for _ in range(SECOND.get(when, 0)):
            n = len(halves)
            up, down = pl.ds(2 * n, 2), pl.ds(6 - 2 * n, 2)
            for copy in started[n]:
                copy.wait_recv()
            halves.append((hop(g.at[left_, up], g.at[left_, up], right, 8 + n), hop(g.at[right, down], g.at[right, down], left_, 10 + n)))

    gather(0)
    own = pltpu.make_async_copy(x_ref, g.at[orb], s4)
    own.start()

    q_of = lax.broadcasted_iota(jnp.int32, (HALF, 16), 0)
    pick = (q_of % 32 // 8 * 4 + q_of % 4 == lax.broadcasted_iota(jnp.int32, (HALF, 16), 1)).astype(bf16)
    i0 = lax.broadcasted_iota(jnp.int32, (HALF, HALF), 0)
    i1 = lax.broadcasted_iota(jnp.int32, (HALF, HALF), 1)
    same = (i0 // 32 == i1 // 32) & (i0 % 8 // 4 == i1 % 8 // 4)
    weight = w_ref[...]
    high = weight.astype(bf16)
    wide_w = []
    for part in (high, (weight - high.astype(f32)).astype(bf16)):
        z = jnp.dot(pick, part, preferred_element_type=f32).astype(bf16)
        z = lax.dot_general(z, pick, (((1,), (1,)), ((), ())), preferred_element_type=f32)
        wide_w.append(jnp.where(same, z, 0.0).astype(bf16))
    wv[...] = jnp.concatenate([wide_w[0], wide_w[1], wide_w[0]], axis=1)

    low = me % HALF
    perm = jnp.where(i0 == (i1 ^ low), 1.0, 0.0).astype(bf16)

    arrived = []
    for step in ORDER:
        a = (orb + NORB - step) % NORB
        count = K - 1 if step == 0 else K
        block = rcv.at[0, pl.ds(0, count)]
        arrived.append(pltpu.make_async_remote_copy(block, block, s1.at[step], r1.at[step], device_id=(wide, orb)))
        arrived[-1].wait_recv()

        def store(r, v):
            rg[a, r] = tile_of(v)

        fft64(lambda k: both_parts(rcv[a, k]), store, mid, 1)
        gather(len(arrived))
        for n in range(2):
            block = rg[a, n * 32 : (n + 1) * 32].reshape(32 * 16, HALF)
            out = jnp.dot(block, perm, preferred_element_type=f32)
            mir[a, n * 32 : (n + 1) * 32] = out.astype(bf16).reshape(32, 16, HALF)

    swap = (lax.broadcasted_iota(jnp.int32, (8, HALF), 0) * 0 + me // HALF) == 1

    def four_sites(first):
        prod_re, prod_im, owns = [], [], []
        for n in range(4):
            r = first + n
            back = (K - r) % K
            for a in range(4):
                u = both_parts(rg[a, r])
                v = both_parts(mir[a, back])
                v = tuple(jnp.where(swap, pltpu.roll(z, 4, 0), z) for z in v)
                prod_re.append(u[0] * v[0] - u[1] * v[1])
                prod_im.append(u[0] * v[1] + u[1] * v[0])
        prod = jnp.concatenate([jnp.concatenate(prod_re, axis=0), jnp.concatenate(prod_im, axis=0)], axis=1)
        high = prod.astype(bf16)
        rest = (prod - high.astype(f32)).astype(bf16)
        return jnp.dot(wv[...], jnp.concatenate([high, high, rest], axis=0), preferred_element_type=f32)

    def sites(i, carry):
        bubbles = [four_sites(i * 16 + m * 4) for m in range(4)]
        for m in range(4):
            for n in range(4):
                r = i * 16 + m * 4 + n
                for a in range(4):
                    row = (n * 4 + a) * 8
                    re, im = bubbles[m][row : row + 8, :HALF], bubbles[m][row : row + 8, HALF:]
                    u = both_parts(rg[a, r])
                    self_real[0, r * NORB + a] = u[0] * re - u[1] * im
                    self_real[1, r * NORB + a] = u[0] * im + u[1] * re
        return carry

    lax.fori_loop(0, K // 16, sites, 0)

    gather(5)

    for turn_n, step in enumerate(ORDER):
        a = (orb + step) % NORB

        def store(k, v):
            snd2[k * NORB + a] = tile_of(v)

        fft64(lambda r: (self_real[0, r * NORB + a], self_real[1, r * NORB + a]), store, mid, -1)

        def send_back(n, carry):
            k = lax.rem(wide + n, K)
            pltpu.make_async_remote_copy(
                snd2.at[k * NORB + a], rcv2.at[orb, wide], s3.at[step], r3.at[step], device_id=(k, a)
            ).start()
            return carry

        lax.fori_loop(1 if step == 0 else 0, K, send_back, 0)
        gather(6 + turn_n)
    rcv2[orb, wide] = snd2[me]

    own.wait()
    for copy in sum(started[2:] + halves, ()):
        copy.wait_recv()
    ge, gt = i0 >= i1, i0 > i1

    def operands(i, carry):
        c, bp = i // 2, i % 2
        for half in range(2):
            b = bp * 2 + half
            lanes = slice(half * HALF, (half + 1) * HALF)
            for part in range(2):
                def m(block):
                    return pl.ds(pl.multiple_of(block * 8 * HALF + (c * 2 + part) * HALF, HALF), HALF)

                own_g = g[c, part * 4 + b].astype(f32)
                adjoint = g[b, part * 4 + c].astype(f32).T
                if part:
                    adjoint = -adjoint
                for n in range(2):
                    blk = slice(n * HALF, (n + 1) * HALF)
                    x, y = own_g[blk, blk], adjoint[blk, blk]
                    rhs[bp, m((R00, R11)[n]), lanes] = jnp.where(ge, x, 0.0).astype(bf16)
                    rhs[bp, m((L00, L11)[n]), lanes] = jnp.where(ge, jnp.where(gt, -y, 0.0), x).astype(bf16)
                    rhs[bp, m((A00, A11)[n]), lanes] = jnp.where(gt, 0.0, y).astype(bf16)
                rhs[bp, m(R10), lanes] = own_g[HALF:, :HALF].astype(bf16)
                rhs[bp, m(L01), lanes] = own_g[:HALF, HALF:].astype(bf16)
                rhs[bp, m(A01), lanes] = adjoint[:HALF, HALF:].astype(bf16)
        return carry

    lax.fori_loop(0, 8, operands, 0)

    returned = []
    for step in ORDER:
        count = K - 1 if step == 0 else K
        block = rcv2.at[0, pl.ds(0, count)]
        returned.append(pltpu.make_async_remote_copy(block, block, s3.at[step], r3.at[step], device_id=(wide, orb)))
        returned[-1].wait_recv()
        plane = (orb + NORB - step) % NORB

        def spread(i, carry):
            for n in range(4):
                w = i * 4 + n
                e = w * NORB + plane
                re, im = both_parts(rcv2[plane, w])
                rows[pl.ds(e, 8, stride=STEP), :] = re
                rows[pl.ds(8 * STEP + e, 8, stride=STEP), :] = im
            return carry

        lax.fori_loop(0, K // 4, spread, 0)

    def left(c, carry):
        for h in range(2):
            for part in range(2):
                x = shear(rows[pl.ds(pl.multiple_of((part * 8 + h * 4 + c) * STEP, 8), NT), :], h)
                top, low_half = x[:HALF], x[HALF:]
                if h == 0:
                    placed = ((0, 1, jnp.where(ge, top, 0.0)), (0, 0, jnp.where(ge, 0.0, top)), (1, 0, low_half), (1, 3, low_half))
                else:
                    placed = ((0, 2, top), (1, 2, jnp.where(ge, low_half, 0.0)), (1, 1, jnp.where(ge, 0.0, low_half)))
                for t, n, z in placed:
                    same = pl.multiple_of(n * 8 * HALF + (c * 2 + part) * HALF, HALF)
                    other = pl.multiple_of(n * 8 * HALF + (c * 2 + 1 - part) * HALF, HALF)
                    lhs[t, :HALF, pl.ds(same, HALF)] = (-z if part else z).astype(bf16)
                    lhs[t, HALF:, pl.ds(other, HALF)] = z.astype(bf16)
        return carry

    lax.fori_loop(0, NORB, left, 0)

    def products(bp, carry):
        def dot(t, first, block, count=1):
            z = lhs[t, :, first * 8 * HALF : (first + count) * 8 * HALF]
            return jnp.dot(z, rhs[bp, block * 8 * HALF : (block + count) * 8 * HALF], preferred_element_type=f32)

        mask = jnp.concatenate([jnp.concatenate([ge, ge], axis=0)] * 2, axis=1)
        quarters = {
            (0, 0): jnp.where(mask, dot(0, 1, R00), dot(0, 0, A00, 2)),
            (0, 1): dot(0, 0, A01, 3),
            (1, 0): dot(1, 2, R10, 2),
            (1, 1): jnp.where(mask, dot(1, 2, R11), dot(1, 0, L01, 3)),
        }
        for (t, u), z in quarters.items():
            z = z.astype(bf16)
            for part in range(2):
                for half in range(2):
                    o_ref[part * 4 + bp * 2 + half, t * HALF : (t + 1) * HALF, u * HALF : (u + 1) * HALF] = z[
                        part * HALF : (part + 1) * HALF, half * HALF : (half + 1) * HALF
                    ]
        return carry

    lax.fori_loop(0, 2, products, 0)

    for copy in arrived + list(sum(started + halves, ())) + returned:
        copy.wait_send()


def local(green_packed, bubble_weight, tile_owner, pairing):
    planes = green_packed.reshape(8, NT, NT)
    vmem = pl.BlockSpec(memory_space=pltpu.VMEM)
    dma = pltpu.SemaphoreType.DMA
    out = pl.pallas_call(
        kernel,
        out_shape=jax.ShapeDtypeStruct((8, NT, NT), bf16),
        in_specs=[vmem, vmem],
        out_specs=vmem,
        scratch_shapes=[
            pltpu.VMEM((16 * STEP, HALF), f32),
            pltpu.VMEM((NDEV, 16, HALF), bf16),
            pltpu.VMEM((NORB, K, 16, HALF), bf16),
            pltpu.VMEM((2, K, 8, HALF), f32),
            pltpu.VMEM((NORB, K, 16, HALF), bf16),
            pltpu.VMEM((NORB, K, 16, HALF), bf16),
            pltpu.VMEM((2, NDEV, 8, HALF), f32),
            pltpu.VMEM((HALF, 3 * HALF), bf16),
            pltpu.VMEM((NDEV, 16, HALF), bf16),
            pltpu.VMEM((NORB, K, 16, HALF), bf16),
            pltpu.VMEM((NORB, 8, NT, NT), bf16),
            pltpu.VMEM((2, 72 * HALF, NT), bf16),
            pltpu.VMEM((2, NT, 32 * HALF), bf16),
        ]
        + [dma((4,))] * 2
        + [dma((12,))] * 2
        + [dma((4,))] * 2
        + [dma],
        compiler_params=pltpu.CompilerParams(has_side_effects=True, collective_id=0, vmem_limit_bytes=38 << 20),
        cost_estimate=pl.CostEstimate(flops=7 * 10**9, bytes_accessed=2 << 20, transcendentals=0),
    )(planes, bubble_weight)
    return out.reshape(green_packed.shape) * jnp.asarray(NT ** (-0.5), bf16)


def solution(mesh):
    return jax.shard_map(
        local,
        mesh=mesh,
        in_specs=(P(None, "wide", "orb", None, None), P(), P(), P()),
        out_specs=P(None, "wide", "orb", None, None),
        check_vma=False,
    )
```

```python
import functools
import math

import jax
import jax.numpy as jnp
from jax import lax
from jax.experimental import pallas as pl
from jax.experimental.pallas import tpu as pltpu
from jax.sharding import PartitionSpec as P

NORB = 4
NT = 256
K = 64
HALF = 128
NDEV = 256
STEP = 264
ORDER = (2, 1, 3, 0)
FIRST = {0: 4}
SECOND = {4: 2}

f32 = jnp.float32
bf16 = jnp.bfloat16

R10, R00, R11, A00, L00, A01, L01, A11, L11 = range(9)


def shear(x, h):
    lane = lax.broadcasted_iota(jnp.int32, (NT, HALF), 1)
    if h:
        x = jnp.concatenate([x[HALF:], x[:HALF]], axis=0)
    for bit in (6, 5, 4, 3):
        m = 1 << bit
        y = x.reshape(NT // (2 * m), 2, m, HALF)
        swapped = jnp.concatenate([y[:, 1:2], y[:, 0:1]], axis=1).reshape(NT, HALF)
        x = jnp.where((lane & m) != 0, swapped, x)
    lane = lax.broadcasted_iota(jnp.int32, (NT // 8, 8, HALF), 2)
    row = lax.broadcasted_iota(jnp.int32, (NT // 8, 8, HALF), 1)
    x = x.reshape(NT // 8, 8, HALF)
    for bit in (2, 1, 0):
        m = 1 << bit
        swapped = pltpu.roll(x, m, 1)
        if bit < 2:
            swapped = jnp.where((row & m) != 0, swapped, pltpu.roll(x, 8 - m, 1))
        x = jnp.where((lane & m) != 0, swapped, x)
    return x.reshape(NT, HALF)


def add(u, v):
    return (u[0] + v[0], u[1] + v[1])


def sub(u, v):
    return (u[0] - v[0], u[1] - v[1])


def times(u, cr, ci):
    return (u[0] * cr - u[1] * ci, u[0] * ci + u[1] * cr)


def turn(u, sign):
    return (-u[1], u[0]) if sign > 0 else (u[1], -u[0])


def fft4(a, b, c, d, sign):
    t0, t1, t2, t3 = add(a, c), sub(a, c), add(b, d), turn(sub(b, d), sign)
    return [add(t0, t2), add(t1, t3), sub(t0, t2), sub(t1, t3)]


def fft8(x, sign):
    even = fft4(x[0], x[2], x[4], x[6], sign)
    odd = fft4(x[1], x[3], x[5], x[7], sign)
    c = math.sqrt(0.5)
    odd = [
        odd[0],
        ((odd[1][0] - sign * odd[1][1]) * c, (sign * odd[1][0] + odd[1][1]) * c),
        turn(odd[2], sign),
        ((-odd[3][0] - sign * odd[3][1]) * c, (sign * odd[3][0] - odd[3][1]) * c),
    ]
    return [add(e, o) for e, o in zip(even, odd)] + [sub(e, o) for e, o in zip(even, odd)]


def fft64(load, store, mid, sign):
    for k2 in range(8):
        y = fft8([load(8 * k1 + k2) for k1 in range(8)], sign)
        for r1 in range(8):
            v = y[r1]
            angle = 2.0 * math.pi * k2 * r1 / 64
            cr, ci = 0.125 * math.cos(angle), sign * 0.125 * math.sin(angle)
            v = times(v, cr, ci) if k2 * r1 else (v[0] * 0.125, v[1] * 0.125)
            mid[0, r1 * 8 + k2] = v[0]
            mid[1, r1 * 8 + k2] = v[1]
    for r1 in range(8):
        y = fft8([(mid[0, r1 * 8 + k2], mid[1, r1 * 8 + k2]) for k2 in range(8)], sign)
        for r2 in range(8):
            store(r1 + 8 * r2, y[r2])


def both_parts(tile):
    x = tile.astype(f32)
    return (x[:8], x[8:])


def tile_of(v):
    return jnp.concatenate([v[0], v[1]], axis=0).astype(bf16)


def kernel(
    x_ref, w_ref, o_ref, rows, snd, rcv, mid, rg, mir, self_real, wv, snd2, rcv2, g, rhs, lhs, s1, r1, s2, r2, s3, r3, s4
):
    orb = lax.axis_index("orb")
    wide = lax.axis_index("wide")
    me = wide * NORB + orb

    def place(d):
        return (d // NORB, d % NORB)

    barrier = pltpu.get_barrier_semaphore()
    planes = [lax.rem(orb + step, NORB) for step in range(NORB)]

    def shear_plane(p, carry):
        for n in range(8):
            there = lax.rem(wide + p * 8 + n, K)
            for step in range(NORB):

                def greet(there=there, step=step):
                    device = (there, planes[step])
                    pl.semaphore_signal(barrier, inc=1, device_id=device, device_id_type=pl.DeviceIdType.MESH)

                if n or step:
                    greet()
                else:
                    pl.when(p > 0)(greet)

        c, b = p // 4, p % 4
        for h in range(2):
            x = x_ref[p, :, h * HALF : (h + 1) * HALF].astype(f32)
            rows[pl.ds(pl.multiple_of((c * 8 + h * 4 + b) * STEP, 8), NT), :] = shear(x, h)
        return carry

    lax.fori_loop(0, 8, shear_plane, 0)

    def make_tile(e):
        snd[e] = tile_of((rows[pl.ds(e, 8, stride=STEP), :], rows[pl.ds(8 * STEP + e, 8, stride=STEP), :]))

    def pack(step, i, carry):
        for n in range(8):
            make_tile((i * 8 + n) * NORB + planes[step])
        return carry

    def send(step, i, carry):
        there = lax.rem(wide + i, K)
        plane = planes[step]
        d = there * NORB + plane
        pltpu.make_async_remote_copy(snd.at[d], rcv.at[orb, wide], s1.at[step], r1.at[step], device_id=(there, plane)).start()
        return carry

    for step in ORDER:
        lax.fori_loop(0, K // 8, functools.partial(pack, step), 0)
        if step == ORDER[0]:
            pl.semaphore_wait(barrier, NDEV - 1)
        lax.fori_loop(0 if step else 1, K, functools.partial(send, step), 0)
    rcv[orb, wide] = snd[me]

    right, left_ = (orb + 1) % NORB, (orb + 3) % NORB
    started, halves = [], []

    def hop(source, planes, target, n):
        copy = pltpu.make_async_remote_copy(source, planes, s2.at[n], r2.at[n], device_id=(wide, target))
        copy.start()
        return copy

    def gather(when):
        for _ in range(FIRST.get(when, 0)):
            n = len(started)
            up, down = pl.ds(2 * n, 2), pl.ds(6 - 2 * n, 2)
            started.append((hop(x_ref.at[up], g.at[orb, up], right, n), hop(x_ref.at[down], g.at[orb, down], left_, 4 + n)))
        for _ in range(SECOND.get(when, 0)):
            n = len(halves)
            up, down = pl.ds(2 * n, 2), pl.ds(6 - 2 * n, 2)
            for copy in started[n]:
                copy.wait_recv()
            halves.append((hop(g.at[left_, up], g.at[left_, up], right, 8 + n), hop(g.at[right, down], g.at[right, down], left_, 10 + n)))

    gather(0)
    own = pltpu.make_async_copy(x_ref, g.at[orb], s4)
    own.start()

    q_of = lax.broadcasted_iota(jnp.int32, (HALF, 16), 0)
    pick = (q_of % 32 // 8 * 4 + q_of % 4 == lax.broadcasted_iota(jnp.int32, (HALF, 16), 1)).astype(bf16)
    i0 = lax.broadcasted_iota(jnp.int32, (HALF, HALF), 0)
    i1 = lax.broadcasted_iota(jnp.int32, (HALF, HALF), 1)
    same = (i0 // 32 == i1 // 32) & (i0 % 8 // 4 == i1 % 8 // 4)
    weight = w_ref[...]
    high = weight.astype(bf16)
    wide_w = []
    for part in (high, (weight - high.astype(f32)).astype(bf16)):
        z = jnp.dot(pick, part, preferred_element_type=f32).astype(bf16)
        z = lax.dot_general(z, pick, (((1,), (1,)), ((), ())), preferred_element_type=f32)
        wide_w.append(jnp.where(same, z, 0.0).astype(bf16))
    wv[...] = jnp.concatenate([wide_w[0], wide_w[1], wide_w[0]], axis=1)

    low = me % HALF
    perm = jnp.where(i0 == (i1 ^ low), 1.0, 0.0).astype(bf16)

    arrived = []
    for step in ORDER:
        a = (orb + NORB - step) % NORB
        count = K - 1 if step == 0 else K
        block = rcv.at[0, pl.ds(0, count)]
        arrived.append(pltpu.make_async_remote_copy(block, block, s1.at[step], r1.at[step], device_id=(wide, orb)))
        arrived[-1].wait_recv()

        def store(r, v):
            rg[a, r] = tile_of(v)

        fft64(lambda k: both_parts(rcv[a, k]), store, mid, 1)
        gather(len(arrived))
        for n in range(2):
            block = rg[a, n * 32 : (n + 1) * 32].reshape(32 * 16, HALF)
            out = jnp.dot(block, perm, preferred_element_type=f32)
            mir[a, n * 32 : (n + 1) * 32] = out.astype(bf16).reshape(32, 16, HALF)

    swap = (lax.broadcasted_iota(jnp.int32, (8, HALF), 0) * 0 + me // HALF) == 1

    def four_sites(first):
        prod_re, prod_im, owns = [], [], []
        for n in range(4):
            r = first + n
            back = (K - r) % K
            for a in range(4):
                u = both_parts(rg[a, r])
                v = both_parts(mir[a, back])
                v = tuple(jnp.where(swap, pltpu.roll(z, 4, 0), z) for z in v)
                prod_re.append(u[0] * v[0] - u[1] * v[1])
                prod_im.append(u[0] * v[1] + u[1] * v[0])
        prod = jnp.concatenate([jnp.concatenate(prod_re, axis=0), jnp.concatenate(prod_im, axis=0)], axis=1)
        high = prod.astype(bf16)
        rest = (prod - high.astype(f32)).astype(bf16)
        return jnp.dot(wv[...], jnp.concatenate([high, high, rest], axis=0), preferred_element_type=f32)

    def sites(i, carry):
        bubbles = [four_sites(i * 16 + m * 4) for m in range(4)]
        for m in range(4):
            for n in range(4):
                r = i * 16 + m * 4 + n
                for a in range(4):
                    row = (n * 4 + a) * 8
                    re, im = bubbles[m][row : row + 8, :HALF], bubbles[m][row : row + 8, HALF:]
                    u = both_parts(rg[a, r])
                    self_real[0, r * NORB + a] = u[0] * re - u[1] * im
                    self_real[1, r * NORB + a] = u[0] * im + u[1] * re
        return carry

    lax.fori_loop(0, K // 16, sites, 0, unroll=True)

    gather(5)

    for turn_n, step in enumerate(ORDER):
        a = (orb + step) % NORB

        def store(k, v):
            snd2[k * NORB + a] = tile_of(v)

        fft64(lambda r: (self_real[0, r * NORB + a], self_real[1, r * NORB + a]), store, mid, -1)

        def send_back(n, carry):
            k = lax.rem(wide + n, K)
            pltpu.make_async_remote_copy(
                snd2.at[k * NORB + a], rcv2.at[orb, wide], s3.at[step], r3.at[step], device_id=(k, a)
            ).start()
            return carry

        lax.fori_loop(1 if step == 0 else 0, K, send_back, 0)
        gather(6 + turn_n)
    rcv2[orb, wide] = snd2[me]

    own.wait()
    for copy in sum(started[2:] + halves, ()):
        copy.wait_recv()
    ge, gt = i0 >= i1, i0 > i1

    def operands(i, carry):
        c, bp = i // 2, i % 2
        for half in range(2):
            b = bp * 2 + half
            lanes = slice(half * HALF, (half + 1) * HALF)
            for part in range(2):
                def m(block):
                    return pl.ds(pl.multiple_of(block * 8 * HALF + (c * 2 + part) * HALF, HALF), HALF)

                own_g = g[c, part * 4 + b].astype(f32)
                adjoint = g[b, part * 4 + c].astype(f32).T
                if part:
                    adjoint = -adjoint
                for n in range(2):
                    blk = slice(n * HALF, (n + 1) * HALF)
                    x, y = own_g[blk, blk], adjoint[blk, blk]
                    rhs[bp, m((R00, R11)[n]), lanes] = jnp.where(ge, x, 0.0).astype(bf16)
                    rhs[bp, m((L00, L11)[n]), lanes] = jnp.where(ge, jnp.where(gt, -y, 0.0), x).astype(bf16)
                    rhs[bp, m((A00, A11)[n]), lanes] = jnp.where(gt, 0.0, y).astype(bf16)
                rhs[bp, m(R10), lanes] = own_g[HALF:, :HALF].astype(bf16)
                rhs[bp, m(L01), lanes] = own_g[:HALF, HALF:].astype(bf16)
                rhs[bp, m(A01), lanes] = adjoint[:HALF, HALF:].astype(bf16)
        return carry

    lax.fori_loop(0, 8, operands, 0)

    returned = []
    for step in ORDER:
        count = K - 1 if step == 0 else K
        block = rcv2.at[0, pl.ds(0, count)]
        returned.append(pltpu.make_async_remote_copy(block, block, s3.at[step], r3.at[step], device_id=(wide, orb)))
        returned[-1].wait_recv()
        plane = (orb + NORB - step) % NORB

        def spread(i, carry):
            for n in range(4):
                w = i * 4 + n
                e = w * NORB + plane
                re, im = both_parts(rcv2[plane, w])
                rows[pl.ds(e, 8, stride=STEP), :] = re
                rows[pl.ds(8 * STEP + e, 8, stride=STEP), :] = im
            return carry

        lax.fori_loop(0, K // 4, spread, 0)

    def left(c, carry):
        for h in range(2):
            for part in range(2):
                x = shear(rows[pl.ds(pl.multiple_of((part * 8 + h * 4 + c) * STEP, 8), NT), :], h)
                top, low_half = x[:HALF], x[HALF:]
                if h == 0:
                    placed = ((0, 1, jnp.where(ge, top, 0.0)), (0, 0, jnp.where(ge, 0.0, top)), (1, 0, low_half), (1, 3, low_half))
                else:
                    placed = ((0, 2, top), (1, 2, jnp.where(ge, low_half, 0.0)), (1, 1, jnp.where(ge, 0.0, low_half)))
                for t, n, z in placed:
                    same = pl.multiple_of(n * 8 * HALF + (c * 2 + part) * HALF, HALF)
                    other = pl.multiple_of(n * 8 * HALF + (c * 2 + 1 - part) * HALF, HALF)
                    lhs[t, :HALF, pl.ds(same, HALF)] = (-z if part else z).astype(bf16)
                    lhs[t, HALF:, pl.ds(other, HALF)] = z.astype(bf16)
        return carry

    lax.fori_loop(0, NORB, left, 0, unroll=True)

    def products(bp, carry):
        def dot(t, first, block, count=1):
            z = lhs[t, :, first * 8 * HALF : (first + count) * 8 * HALF]
            return jnp.dot(z, rhs[bp, block * 8 * HALF : (block + count) * 8 * HALF], preferred_element_type=f32)

        mask = jnp.concatenate([jnp.concatenate([ge, ge], axis=0)] * 2, axis=1)
        quarters = {
            (0, 0): jnp.where(mask, dot(0, 1, R00), dot(0, 0, A00, 2)),
            (0, 1): dot(0, 0, A01, 3),
            (1, 0): dot(1, 2, R10, 2),
            (1, 1): jnp.where(mask, dot(1, 2, R11), dot(1, 0, L01, 3)),
        }
        for (t, u), z in quarters.items():
            z = z.astype(bf16)
            for part in range(2):
                for half in range(2):
                    o_ref[part * 4 + bp * 2 + half, t * HALF : (t + 1) * HALF, u * HALF : (u + 1) * HALF] = z[
                        part * HALF : (part + 1) * HALF, half * HALF : (half + 1) * HALF
                    ]
        return carry

    lax.fori_loop(0, 2, products, 0, unroll=True)

    for copy in arrived + list(sum(started + halves, ())) + returned:
        copy.wait_send()


def local(green_packed, bubble_weight, tile_owner, pairing):
    planes = green_packed.reshape(8, NT, NT)
    vmem = pl.BlockSpec(memory_space=pltpu.VMEM)
    dma = pltpu.SemaphoreType.DMA
    out = pl.pallas_call(
        kernel,
        out_shape=jax.ShapeDtypeStruct((8, NT, NT), bf16),
        in_specs=[vmem, vmem],
        out_specs=vmem,
        scratch_shapes=[
            pltpu.VMEM((16 * STEP, HALF), f32),
            pltpu.VMEM((NDEV, 16, HALF), bf16),
            pltpu.VMEM((NORB, K, 16, HALF), bf16),
            pltpu.VMEM((2, K, 8, HALF), f32),
            pltpu.VMEM((NORB, K, 16, HALF), bf16),
            pltpu.VMEM((NORB, K, 16, HALF), bf16),
            pltpu.VMEM((2, NDEV, 8, HALF), f32),
            pltpu.VMEM((HALF, 3 * HALF), bf16),
            pltpu.VMEM((NDEV, 16, HALF), bf16),
            pltpu.VMEM((NORB, K, 16, HALF), bf16),
            pltpu.VMEM((NORB, 8, NT, NT), bf16),
            pltpu.VMEM((2, 72 * HALF, NT), bf16),
            pltpu.VMEM((2, NT, 32 * HALF), bf16),
        ]
        + [dma((4,))] * 2
        + [dma((12,))] * 2
        + [dma((4,))] * 2
        + [dma],
        compiler_params=pltpu.CompilerParams(has_side_effects=True, collective_id=0, vmem_limit_bytes=38 << 20),
        cost_estimate=pl.CostEstimate(flops=7 * 10**9, bytes_accessed=2 << 20, transcendentals=0),
    )(planes, bubble_weight)
    return out.reshape(green_packed.shape) * jnp.asarray(NT ** (-0.5), bf16)


def solution(mesh):
    return jax.shard_map(
        local,
        mesh=mesh,
        in_specs=(P(None, "wide", "orb", None, None), P(), P(), P()),
        out_specs=P(None, "wide", "orb", None, None),
        check_vma=False,
    )
```

```python
import functools
import math

import jax
import jax.numpy as jnp
from jax import lax
from jax.experimental import pallas as pl
from jax.experimental.pallas import tpu as pltpu
from jax.sharding import PartitionSpec as P

NORB = 4
NT = 256
K = 64
HALF = 128
NDEV = 256
STEP = 264
ORDER = (2, 1, 3, 0)
FIRST = {0: 4}
SECOND = {3: 1, 4: 1}

f32 = jnp.float32
bf16 = jnp.bfloat16

R10, R00, R11, A00, L00, A01, L01, A11, L11 = range(9)


def shear(x, h):
    lane = lax.broadcasted_iota(jnp.int32, (NT, HALF), 1)
    if h:
        x = jnp.concatenate([x[HALF:], x[:HALF]], axis=0)
    for bit in (6, 5, 4, 3):
        m = 1 << bit
        y = x.reshape(NT // (2 * m), 2, m, HALF)
        swapped = jnp.concatenate([y[:, 1:2], y[:, 0:1]], axis=1).reshape(NT, HALF)
        x = jnp.where((lane & m) != 0, swapped, x)
    lane = lax.broadcasted_iota(jnp.int32, (NT // 8, 8, HALF), 2)
    row = lax.broadcasted_iota(jnp.int32, (NT // 8, 8, HALF), 1)
    x = x.reshape(NT // 8, 8, HALF)
    for bit in (2, 1, 0):
        m = 1 << bit
        swapped = pltpu.roll(x, m, 1)
        if bit < 2:
            swapped = jnp.where((row & m) != 0, swapped, pltpu.roll(x, 8 - m, 1))
        x = jnp.where((lane & m) != 0, swapped, x)
    return x.reshape(NT, HALF)


def add(u, v):
    return (u[0] + v[0], u[1] + v[1])


def sub(u, v):
    return (u[0] - v[0], u[1] - v[1])


def times(u, cr, ci):
    return (u[0] * cr - u[1] * ci, u[0] * ci + u[1] * cr)


def turn(u, sign):
    return (-u[1], u[0]) if sign > 0 else (u[1], -u[0])


def fft4(a, b, c, d, sign):
    t0, t1, t2, t3 = add(a, c), sub(a, c), add(b, d), turn(sub(b, d), sign)
    return [add(t0, t2), add(t1, t3), sub(t0, t2), sub(t1, t3)]


def fft8(x, sign):
    even = fft4(x[0], x[2], x[4], x[6], sign)
    odd = fft4(x[1], x[3], x[5], x[7], sign)
    c = math.sqrt(0.5)
    odd = [
        odd[0],
        ((odd[1][0] - sign * odd[1][1]) * c, (sign * odd[1][0] + odd[1][1]) * c),
        turn(odd[2], sign),
        ((-odd[3][0] - sign * odd[3][1]) * c, (sign * odd[3][0] - odd[3][1]) * c),
    ]
    return [add(e, o) for e, o in zip(even, odd)] + [sub(e, o) for e, o in zip(even, odd)]


def fft64(load, store, mid, sign):
    for k2 in range(8):
        y = fft8([load(8 * k1 + k2) for k1 in range(8)], sign)
        for r1 in range(8):
            v = y[r1]
            angle = 2.0 * math.pi * k2 * r1 / 64
            cr, ci = 0.125 * math.cos(angle), sign * 0.125 * math.sin(angle)
            v = times(v, cr, ci) if k2 * r1 else (v[0] * 0.125, v[1] * 0.125)
            mid[0, r1 * 8 + k2] = v[0]
            mid[1, r1 * 8 + k2] = v[1]
    for r1 in range(8):
        y = fft8([(mid[0, r1 * 8 + k2], mid[1, r1 * 8 + k2]) for k2 in range(8)], sign)
        for r2 in range(8):
            store(r1 + 8 * r2, y[r2])


def both_parts(tile):
    x = tile.astype(f32)
    return (x[:8], x[8:])


def tile_of(v):
    return jnp.concatenate([v[0], v[1]], axis=0).astype(bf16)


def kernel(
    x_ref, w_ref, o_ref, rows, snd, rcv, mid, rg, mir, self_real, wv, snd2, rcv2, g, rhs, lhs, s1, r1, s2, r2, s3, r3, s4
):
    orb = lax.axis_index("orb")
    wide = lax.axis_index("wide")
    me = wide * NORB + orb

    def place(d):
        return (d // NORB, d % NORB)

    barrier = pltpu.get_barrier_semaphore()
    planes = [lax.rem(orb + step, NORB) for step in range(NORB)]

    def shear_plane(p, carry):
        for n in range(8):
            there = lax.rem(wide + p * 8 + n, K)
            for step in range(NORB):

                def greet(there=there, step=step):
                    device = (there, planes[step])
                    pl.semaphore_signal(barrier, inc=1, device_id=device, device_id_type=pl.DeviceIdType.MESH)

                if n or step:
                    greet()
                else:
                    pl.when(p > 0)(greet)

        c, b = p // 4, p % 4
        for h in range(2):
            x = x_ref[p, :, h * HALF : (h + 1) * HALF].astype(f32)
            rows[pl.ds(pl.multiple_of((c * 8 + h * 4 + b) * STEP, 8), NT), :] = shear(x, h)
        return carry

    lax.fori_loop(0, 8, shear_plane, 0)

    def make_tile(e):
        snd[e] = tile_of((rows[pl.ds(e, 8, stride=STEP), :], rows[pl.ds(8 * STEP + e, 8, stride=STEP), :]))

    def pack(step, i, carry):
        for n in range(8):
            make_tile((i * 8 + n) * NORB + planes[step])
        return carry

    def send(step, i, carry):
        there = lax.rem(wide + i, K)
        plane = planes[step]
        d = there * NORB + plane
        pltpu.make_async_remote_copy(snd.at[d], rcv.at[orb, wide], s1.at[step], r1.at[step], device_id=(there, plane)).start()
        return carry

    for step in ORDER:
        lax.fori_loop(0, K // 8, functools.partial(pack, step), 0)
        if step == ORDER[0]:
            pl.semaphore_wait(barrier, NDEV - 1)
        lax.fori_loop(0 if step else 1, K, functools.partial(send, step), 0)
    rcv[orb, wide] = snd[me]

    right, left_ = (orb + 1) % NORB, (orb + 3) % NORB
    started, halves = [], []

    def hop(source, planes, target, n):
        copy = pltpu.make_async_remote_copy(source, planes, s2.at[n], r2.at[n], device_id=(wide, target))
        copy.start()
        return copy

    def gather(when):
        for _ in range(FIRST.get(when, 0)):
            n = len(started)
            up, down = pl.ds(2 * n, 2), pl.ds(6 - 2 * n, 2)
            started.append((hop(x_ref.at[up], g.at[orb, up], right, n), hop(x_ref.at[down], g.at[orb, down], left_, 4 + n)))
        for _ in range(SECOND.get(when, 0)):
            n = len(halves)
            up, down = pl.ds(2 * n, 2), pl.ds(6 - 2 * n, 2)
            for copy in started[n]:
                copy.wait_recv()
            halves.append((hop(g.at[left_, up], g.at[left_, up], right, 8 + n), hop(g.at[right, down], g.at[right, down], left_, 10 + n)))

    gather(0)
    own = pltpu.make_async_copy(x_ref, g.at[orb], s4)
    own.start()

    q_of = lax.broadcasted_iota(jnp.int32, (HALF, 16), 0)
    pick = (q_of % 32 // 8 * 4 + q_of % 4 == lax.broadcasted_iota(jnp.int32, (HALF, 16), 1)).astype(bf16)
    i0 = lax.broadcasted_iota(jnp.int32, (HALF, HALF), 0)
    i1 = lax.broadcasted_iota(jnp.int32, (HALF, HALF), 1)
    same = (i0 // 32 == i1 // 32) & (i0 % 8 // 4 == i1 % 8 // 4)
    weight = w_ref[...]
    high = weight.astype(bf16)
    wide_w = []
    for part in (high, (weight - high.astype(f32)).astype(bf16)):
        z = jnp.dot(pick, part, preferred_element_type=f32).astype(bf16)
        z = lax.dot_general(z, pick, (((1,), (1,)), ((), ())), preferred_element_type=f32)
        wide_w.append(jnp.where(same, z, 0.0).astype(bf16))
    wv[...] = jnp.concatenate([wide_w[0], wide_w[1], wide_w[0]], axis=1)

    low = me % HALF
    perm = jnp.where(i0 == (i1 ^ low), 1.0, 0.0).astype(bf16)

    arrived = []
    for step in ORDER:
        a = (orb + NORB - step) % NORB
        count = K - 1 if step == 0 else K
        block = rcv.at[0, pl.ds(0, count)]
        arrived.append(pltpu.make_async_remote_copy(block, block, s1.at[step], r1.at[step], device_id=(wide, orb)))
        arrived[-1].wait_recv()

        def store(r, v):
            rg[a, r] = tile_of(v)

        fft64(lambda k: both_parts(rcv[a, k]), store, mid, 1)
        gather(len(arrived))
        for n in range(2):
            block = rg[a, n * 32 : (n + 1) * 32].reshape(32 * 16, HALF)
            out = jnp.dot(block, perm, preferred_element_type=f32)
            mir[a, n * 32 : (n + 1) * 32] = out.astype(bf16).reshape(32, 16, HALF)

    swap = (lax.broadcasted_iota(jnp.int32, (8, HALF), 0) * 0 + me // HALF) == 1

    def four_sites(first):
        prod_re, prod_im, owns = [], [], []
        for n in range(4):
            r = first + n
            back = (K - r) % K
            for a in range(4):
                u = both_parts(rg[a, r])
                v = both_parts(mir[a, back])
                v = tuple(jnp.where(swap, pltpu.roll(z, 4, 0), z) for z in v)
                prod_re.append(u[0] * v[0] - u[1] * v[1])
                prod_im.append(u[0] * v[1] + u[1] * v[0])
        prod = jnp.concatenate([jnp.concatenate(prod_re, axis=0), jnp.concatenate(prod_im, axis=0)], axis=1)
        high = prod.astype(bf16)
        rest = (prod - high.astype(f32)).astype(bf16)
        return jnp.dot(wv[...], jnp.concatenate([high, high, rest], axis=0), preferred_element_type=f32)

    def sites(i, carry):
        bubbles = [four_sites(i * 16 + m * 4) for m in range(4)]
        for m in range(4):
            for n in range(4):
                r = i * 16 + m * 4 + n
                for a in range(4):
                    row = (n * 4 + a) * 8
                    re, im = bubbles[m][row : row + 8, :HALF], bubbles[m][row : row + 8, HALF:]
                    u = both_parts(rg[a, r])
                    self_real[0, r * NORB + a] = u[0] * re - u[1] * im
                    self_real[1, r * NORB + a] = u[0] * im + u[1] * re
        return carry

    lax.fori_loop(0, K // 16, sites, 0, unroll=True)

    gather(5)

    for turn_n, step in enumerate(ORDER):
        a = (orb + step) % NORB

        def store(k, v):
            snd2[k * NORB + a] = tile_of(v)

        fft64(lambda r: (self_real[0, r * NORB + a], self_real[1, r * NORB + a]), store, mid, -1)

        def send_back(n, carry):
            k = lax.rem(wide + n, K)
            pltpu.make_async_remote_copy(
                snd2.at[k * NORB + a], rcv2.at[orb, wide], s3.at[step], r3.at[step], device_id=(k, a)
            ).start()
            return carry

        lax.fori_loop(1 if step == 0 else 0, K, send_back, 0)
        gather(6 + turn_n)
    rcv2[orb, wide] = snd2[me]

    own.wait()
    for copy in sum(started[2:] + halves, ()):
        copy.wait_recv()
    ge, gt = i0 >= i1, i0 > i1

    def operands(i, carry):
        c, bp = i // 2, i % 2
        for half in range(2):
            b = bp * 2 + half
            lanes = slice(half * HALF, (half + 1) * HALF)
            for part in range(2):
                def m(block):
                    return pl.ds(pl.multiple_of(block * 8 * HALF + (c * 2 + part) * HALF, HALF), HALF)

                own_g = g[c, part * 4 + b].astype(f32)
                adjoint = g[b, part * 4 + c].astype(f32).T
                if part:
                    adjoint = -adjoint
                for n in range(2):
                    blk = slice(n * HALF, (n + 1) * HALF)
                    x, y = own_g[blk, blk], adjoint[blk, blk]
                    rhs[bp, m((R00, R11)[n]), lanes] = jnp.where(ge, x, 0.0).astype(bf16)
                    rhs[bp, m((L00, L11)[n]), lanes] = jnp.where(ge, jnp.where(gt, -y, 0.0), x).astype(bf16)
                    rhs[bp, m((A00, A11)[n]), lanes] = jnp.where(gt, 0.0, y).astype(bf16)
                rhs[bp, m(R10), lanes] = own_g[HALF:, :HALF].astype(bf16)
                rhs[bp, m(L01), lanes] = own_g[:HALF, HALF:].astype(bf16)
                rhs[bp, m(A01), lanes] = adjoint[:HALF, HALF:].astype(bf16)
        return carry

    lax.fori_loop(0, 8, operands, 0)

    returned = []
    for step in ORDER:
        count = K - 1 if step == 0 else K
        block = rcv2.at[0, pl.ds(0, count)]
        returned.append(pltpu.make_async_remote_copy(block, block, s3.at[step], r3.at[step], device_id=(wide, orb)))
        returned[-1].wait_recv()
        plane = (orb + NORB - step) % NORB

        def spread(i, carry):
            for n in range(4):
                w = i * 4 + n
                e = w * NORB + plane
                re, im = both_parts(rcv2[plane, w])
                rows[pl.ds(e, 8, stride=STEP), :] = re
                rows[pl.ds(8 * STEP + e, 8, stride=STEP), :] = im
            return carry

        lax.fori_loop(0, K // 4, spread, 0)

    def left(c, carry):
        for h in range(2):
            for part in range(2):
                x = shear(rows[pl.ds(pl.multiple_of((part * 8 + h * 4 + c) * STEP, 8), NT), :], h)
                top, low_half = x[:HALF], x[HALF:]
                if h == 0:
                    placed = ((0, 1, jnp.where(ge, top, 0.0)), (0, 0, jnp.where(ge, 0.0, top)), (1, 0, low_half), (1, 3, low_half))
                else:
                    placed = ((0, 2, top), (1, 2, jnp.where(ge, low_half, 0.0)), (1, 1, jnp.where(ge, 0.0, low_half)))
                for t, n, z in placed:
                    same = pl.multiple_of(n * 8 * HALF + (c * 2 + part) * HALF, HALF)
                    other = pl.multiple_of(n * 8 * HALF + (c * 2 + 1 - part) * HALF, HALF)
                    lhs[t, :HALF, pl.ds(same, HALF)] = (-z if part else z).astype(bf16)
                    lhs[t, HALF:, pl.ds(other, HALF)] = z.astype(bf16)
        return carry

    lax.fori_loop(0, NORB, left, 0, unroll=True)

    def products(bp, carry):
        def dot(t, first, block, count=1):
            z = lhs[t, :, first * 8 * HALF : (first + count) * 8 * HALF]
            return jnp.dot(z, rhs[bp, block * 8 * HALF : (block + count) * 8 * HALF], preferred_element_type=f32)

        mask = jnp.concatenate([jnp.concatenate([ge, ge], axis=0)] * 2, axis=1)
        quarters = {
            (0, 0): jnp.where(mask, dot(0, 1, R00), dot(0, 0, A00, 2)),
            (0, 1): dot(0, 0, A01, 3),
            (1, 0): dot(1, 2, R10, 2),
            (1, 1): jnp.where(mask, dot(1, 2, R11), dot(1, 0, L01, 3)),
        }
        for (t, u), z in quarters.items():
            z = z.astype(bf16)
            for part in range(2):
                for half in range(2):
                    o_ref[part * 4 + bp * 2 + half, t * HALF : (t + 1) * HALF, u * HALF : (u + 1) * HALF] = z[
                        part * HALF : (part + 1) * HALF, half * HALF : (half + 1) * HALF
                    ]
        return carry

    lax.fori_loop(0, 2, products, 0, unroll=True)

    for copy in arrived + list(sum(started + halves, ())) + returned:
        copy.wait_send()


def local(green_packed, bubble_weight, tile_owner, pairing):
    planes = green_packed.reshape(8, NT, NT)
    vmem = pl.BlockSpec(memory_space=pltpu.VMEM)
    dma = pltpu.SemaphoreType.DMA
    out = pl.pallas_call(
        kernel,
        out_shape=jax.ShapeDtypeStruct((8, NT, NT), bf16),
        in_specs=[vmem, vmem],
        out_specs=vmem,
        scratch_shapes=[
            pltpu.VMEM((16 * STEP, HALF), f32),
            pltpu.VMEM((NDEV, 16, HALF), bf16),
            pltpu.VMEM((NORB, K, 16, HALF), bf16),
            pltpu.VMEM((2, K, 8, HALF), f32),
            pltpu.VMEM((NORB, K, 16, HALF), bf16),
            pltpu.VMEM((NORB, K, 16, HALF), bf16),
            pltpu.VMEM((2, NDEV, 8, HALF), f32),
            pltpu.VMEM((HALF, 3 * HALF), bf16),
            pltpu.VMEM((NDEV, 16, HALF), bf16),
            pltpu.VMEM((NORB, K, 16, HALF), bf16),
            pltpu.VMEM((NORB, 8, NT, NT), bf16),
            pltpu.VMEM((2, 72 * HALF, NT), bf16),
            pltpu.VMEM((2, NT, 32 * HALF), bf16),
        ]
        + [dma((4,))] * 2
        + [dma((12,))] * 2
        + [dma((4,))] * 2
        + [dma],
        compiler_params=pltpu.CompilerParams(has_side_effects=True, collective_id=0, vmem_limit_bytes=38 << 20),
        cost_estimate=pl.CostEstimate(flops=7 * 10**9, bytes_accessed=2 << 20, transcendentals=0),
    )(planes, bubble_weight)
    return out.reshape(green_packed.shape) * jnp.asarray(NT ** (-0.5), bf16)


def solution(mesh):
    return jax.shard_map(
        local,
        mesh=mesh,
        in_specs=(P(None, "wide", "orb", None, None), P(), P(), P()),
        out_specs=P(None, "wide", "orb", None, None),
        check_vma=False,
    )
```
